256 devices in a mesh: role: 2 (over y_hi), dp: 8 (over z), tensor: 16 (over x, y_lo, core).
Axes of the slice: x: 4, y: 4 (y_hi: 2, y_lo: 2; y = y_hi * 2 + y_lo), z: 8, core: 2. Of those that a mesh axis runs over, the one named last changes fastest.
Arguments:
- learner_inputs: bfloat16 [16384, 8192], P(('role', 'dp'), 'tensor'), may hold values from -6 to 6
- learner_cotangent: bfloat16 [16384, 5120], P(('role', 'dp'), 'tensor'), may hold values from -0.0625 to 0.0625
- master_weight: float32 [8192, 5120], P('tensor', ('role', 'dp')), may hold values from -5 to 5
- first_moment: float32 [8192, 5120], P('tensor', ('role', 'dp')), may hold values from -3 to 3
- second_moment: float32 [8192, 5120], P('tensor', ('role', 'dp')), may hold values from 0.02 to 1
- query_weight: bfloat16 [5120, 8192], P(None, 'tensor'), may hold values from -0.078125 to 0.078125
- keyval_weight: bfloat16 [5120, 2048], P(None, 'tensor'), may hold values from -0.078125 to 0.078125
- prefix_cache: bfloat16 [64, 512, 2048], P(('role', 'dp'), None, 'tensor'), may hold values from -4000 to 4000
- block_states: bfloat16 [64, 32, 5120], P(('role', 'dp'), None, 'tensor'), may hold values from -50 to 50
- norm_gain: float32 [5120], replicated, may hold values from 0.1 to 1.9
- mask_vector: bfloat16 [5120], replicated, may hold values from -5 to 5
- prefix_lengths: int32 [64], P(('role', 'dp')), may hold values from 128 to 512, as said below
- position_picks: int32 [2, 64, 32], P(None, ('role', 'dp')), may hold values from 0 to 2
Outputs:
- next_states: bfloat16 [64, 32, 5120], P(('role', 'dp'), None, 'tensor')
- new_weight: float32 [8192, 5120], P('tensor', ('role', 'dp'))
- new_first: float32 [8192, 5120], P('tensor', ('role', 'dp'))
- new_second: float32 [8192, 5120], P('tensor', ('role', 'dp'))
The draws below stay inside these ranges and needn't reach their ends.
Inputs may be any that keep to these rules, and one draw needn't show every extreme that they name: `prefix_lengths`: every row has 128 or more valid positions; some row has all 512 and some row exactly 128.
All inputs are finite; a program needn't handle non-finite values.
Results may differ from the reference program's by a relative error of at most 0.025.
Values may be sent and summed in bfloat16 or wider, within the bound.
No kernel may reach another device: no remote copies, remote signals or barrier semaphores. Data moves between devices by JAX's collectives and lax.ppermute only.
A program may use at most 128 MiB of HBM per device.

```python
import math
import jax
import jax.numpy as jnp
from jax import lax

D = 5120
HEADS = 64
HEAD = 128
KV_HEADS = 8
BLOCK = 32
STEPS = 2
PREFIX = 512
QW = 8192
ROWS = 64
TOKENS = 16384


def draw_prefix_cache(key, part):
    key = jax.random.fold_in(key, 11)
    key_noise = jax.random.fold_in(key, 0)
    shape_full = (ROWS, PREFIX, KV_HEADS, 2, HEAD)
    entries = jnp.clip(1.5 * jax.random.normal(key_noise, shape_full, jnp.float32), -8.0, 8.0)
    return entries.reshape(ROWS, PREFIX, KV_HEADS * 2 * HEAD).astype(jnp.bfloat16)


def draw_block_states(key, part):
    key = jax.random.fold_in(key, 12)
    key_noise, key_rows, key_cols = jax.random.split(key, 3)
    shape_full = (ROWS, BLOCK, D)
    entries = jnp.clip(jax.random.normal(key_noise, shape_full, jnp.float32), -5.0, 5.0)
    low_end = 0.3
    high_end = 3.0
    row_scale = jnp.exp(jax.random.uniform(key_rows, (ROWS, BLOCK, 1), jnp.float32, math.log(low_end), math.log(high_end)))
    col_scale = jnp.exp(jax.random.uniform(key_cols, (1, 1, D), jnp.float32, math.log(low_end), math.log(high_end)))
    return (entries * row_scale * col_scale).astype(jnp.bfloat16)


def draw_prefix_lengths(key, part):
    key = jax.random.fold_in(key, 13)
    key_lens, key_top, key_low = jax.random.split(key, 3)
    lengths_drawn = jax.random.randint(key_lens, (ROWS,), PREFIX // 4, PREFIX + 1)
    row_top = jax.random.randint(key_top, (), 0, ROWS)
    row_low = (row_top + jax.random.randint(key_low, (), 1, ROWS)) % ROWS
    row_index = jnp.arange(ROWS)
    lengths_drawn = jnp.where(row_index == row_top, PREFIX, jnp.where(row_index == row_low, PREFIX // 4, lengths_drawn))
    return lengths_drawn.astype(jnp.int32)


def set_ends(array, own_key, smallest, high):
    shape = array.shape
    place = [jax.random.randint(jax.random.fold_in(own_key, axis), (), 0, shape[axis]) for axis in range(len(shape))]
    array = array.at[tuple(place)].set(smallest)
    longest = shape.index(max(shape))
    place[longest] = (place[longest] + 1) % shape[longest]
    return array.at[tuple(place)].set(high)


def spiked(array, own_key, source, target, blocks, factor):
    def block_of(dim):
        return (jnp.arange(array.shape[dim]) // (array.shape[dim] // blocks)).reshape((-1,) + (1,) * (array.ndim - 1 - dim))

    near = jax.random.permutation(own_key, blocks)[block_of(target)]
    second = (block_of(target) + blocks // 2) % blocks
    return jnp.where((block_of(source) == near) | (block_of(source) == second), factor * array, array)


def levels(rng, shape, cuts, low, high):
    def one(dim, shards_of):
        steps = jax.random.uniform(jax.random.fold_in(jax.random.fold_in(rng, 6), dim), (shards_of,), jnp.float32, low / len(cuts), high / len(cuts))
        return jnp.repeat(jnp.exp(steps), shape[dim] // shards_of).reshape((-1,) + (1,) * (len(shape) - dim - 1))

    factor_of = one(*cuts[0])
    for cut in cuts[1:]:
        factor_of = factor_of * one(*cut)
    return factor_of


def noise(stream_key, shape, spread, limit, cuts=(), kind=jnp.bfloat16):
    factor_of = levels(stream_key, shape, cuts, -0.22, 0.18) if cuts else 1.0
    result = jax.random.normal(stream_key, shape, jnp.float32) * spread * factor_of
    return jnp.minimum(jnp.maximum(result, -limit), limit).astype(kind)


def noise_with(rng, extent, deviation, bound, cuts, heavy, kind=jnp.bfloat16):
    values = deviation * jax.random.normal(rng, extent, jnp.float32)
    if cuts:
        values = values * levels(rng, extent, cuts, -0.22, 0.18)
    return jnp.clip(spiked(values, jax.random.fold_in(rng, 3), *heavy), -bound, bound).astype(kind)


def setup_inputs(seed: int = 0) -> dict:
    arg_keys = jax.random.split(jax.random.key(seed), 14)
    return {
        "learner_inputs": noise(arg_keys[0], (TOKENS, QW), 1.0, 6.0, ((0, 16), (1, 16))),
        "learner_cotangent": noise_with(arg_keys[1], (TOKENS, D), TOKENS ** -0.5, 0.0625, ((0, 16), (1, 16)), (0, 1, 16, 2.0)),
        "master_weight": noise(arg_keys[2], (QW, D), 1.0, 5.0, ((0, 16), (1, 16)), jnp.float32),
        "first_moment": noise(arg_keys[3], (QW, D), 0.3, 3.0, ((0, 16), (1, 16)), jnp.float32),
        "second_moment": jnp.clip(jnp.exp(math.log(1.0) - 3.912023 * jax.random.uniform(arg_keys[4], (QW, D), jnp.float32) ** levels(arg_keys[4], (QW, D), ((0, 16), (1, 16)), -0.2, 0.2)), 0.02, 1.0),
        "query_weight": noise(arg_keys[5], (D, QW), D ** -0.5, 0.078125, ((1, 16),)),
        "keyval_weight": noise(arg_keys[6], (D, 2 * KV_HEADS * HEAD), D ** -0.5, 0.078125, ((1, 16),)),
        "prefix_cache": draw_prefix_cache(jax.random.fold_in(arg_keys[13], 71), 0),
        "block_states": draw_block_states(jax.random.fold_in(arg_keys[13], 71), 0),
        "norm_gain": jnp.clip(1.0 + 0.18 * jax.random.normal(arg_keys[9], (D,), jnp.float32), 0.1, 1.9),
        "mask_vector": noise(arg_keys[10], (D,), 1.0, 5.0),
        "prefix_lengths": draw_prefix_lengths(jax.random.fold_in(arg_keys[13], 71), 0),
        "position_picks": set_ends(jax.random.randint(arg_keys[12], (STEPS, ROWS, BLOCK), 0, 3), jax.random.fold_in(arg_keys[12], 1), 0, 2).astype(jnp.int32),
    }


BETA_ONE = 0.9
BETA_TWO = 0.95
ADAM_EPS = 1e-08
LEARN_RATE = 0.5
DECAY_RATE = 0.1
STEP_COUNT = 50
NORM_EPS = 1e-06

def adam_update(gradient, master_weight, first_moment, second_moment):
    first_new = BETA_ONE * first_moment + (1.0 - BETA_ONE) * gradient
    second_new = BETA_TWO * second_moment + (1.0 - BETA_TWO) * gradient * gradient
    first_hat = first_new / (1.0 - BETA_ONE ** STEP_COUNT)
    second_hat = second_new / (1.0 - BETA_TWO ** STEP_COUNT)
    weight_new = master_weight - LEARN_RATE * (first_hat / (jnp.sqrt(second_hat) + ADAM_EPS) + DECAY_RATE * master_weight)
    return (weight_new, first_new, second_new)

def normalize(current_state, norm_gain):
    values = current_state.astype(jnp.float32)
    mean_square = lax.optimization_barrier(jnp.mean(values * values, axis=-1, keepdims=True))
    return (values * lax.rsqrt(mean_square + NORM_EPS) * norm_gain).astype(jnp.bfloat16)

def revise(current_state, update, pick_codes, mask_values):
    values = current_state.astype(jnp.float32)
    pick_cols = pick_codes[..., None]
    masked = jnp.broadcast_to(mask_values.astype(jnp.float32), values.shape)
    return jnp.where(pick_cols == 1, values + update, jnp.where(pick_cols == 2, masked, values)).astype(jnp.bfloat16)

def single_row(operands):
    queries, cache_pair, block_pairs, row_length = operands
    score_scale = HEAD ** (-0.5)
    query_f = queries.astype(jnp.float32)
    cache_keys = cache_pair[:, :, 0].astype(jnp.float32)
    cache_values = cache_pair[:, :, 1].astype(jnp.float32)
    block_keys = block_pairs[:, :, 0].astype(jnp.float32)
    block_values = block_pairs[:, :, 1].astype(jnp.float32)
    prefix_scores = jnp.einsum('bkgh,pkh->kgbp', query_f, cache_keys) * score_scale
    valid_keys = jnp.arange(PREFIX, dtype=jnp.int32) < row_length
    prefix_scores = jnp.where(valid_keys, prefix_scores, -jnp.inf)
    block_scores = jnp.einsum('bkgh,ckh->kgbc', query_f, block_keys) * score_scale
    score_top = jnp.maximum(lax.optimization_barrier(jnp.max(prefix_scores, axis=-1)), lax.optimization_barrier(jnp.max(block_scores, axis=-1)))[..., None]
    prefix_exp = jnp.exp(prefix_scores - score_top)
    block_exp = jnp.exp(block_scores - score_top)
    denom_sum = (lax.optimization_barrier(jnp.sum(prefix_exp, axis=-1)) + lax.optimization_barrier(jnp.sum(block_exp, axis=-1)))[..., None]
    prefix_probs = (prefix_exp / denom_sum).astype(jnp.bfloat16).astype(jnp.float32)
    block_probs = (block_exp / denom_sum).astype(jnp.bfloat16).astype(jnp.float32)
    attended = jnp.einsum('kgbp,pkh->bkgh', prefix_probs, cache_values)
    attended = attended + jnp.einsum('kgbc,ckh->bkgh', block_probs, block_values)
    return attended.astype(jnp.bfloat16).reshape(BLOCK, HEADS * HEAD)

def reference(learner_inputs, learner_cotangent, master_weight, first_moment, second_moment, query_weight, keyval_weight, prefix_cache, block_states, norm_gain, mask_vector, prefix_lengths, position_picks):
    gradient = jnp.dot(learner_inputs.T, learner_cotangent, preferred_element_type=jnp.float32)
    new_weight, new_first, new_second = adam_update(gradient, master_weight, first_moment, second_moment)
    layer_rows = new_weight.astype(jnp.bfloat16)
    group_size = HEADS // KV_HEADS
    cache_pair = prefix_cache.reshape(ROWS, PREFIX, KV_HEADS, 2, HEAD)
    current_state = block_states
    for step_index in range(STEPS):
        normed = normalize(current_state, norm_gain)
        flat_normed = normed.reshape(ROWS * BLOCK, D)
        queries = jnp.dot(flat_normed, query_weight, preferred_element_type=jnp.float32).astype(jnp.bfloat16)
        queries = queries.reshape(ROWS, BLOCK, KV_HEADS, group_size, HEAD)
        block_pairs = jnp.dot(flat_normed, keyval_weight, preferred_element_type=jnp.float32).astype(jnp.bfloat16)
        block_pairs = block_pairs.reshape(ROWS, BLOCK, KV_HEADS, 2, HEAD)
        attended = lax.map(single_row, (queries, cache_pair, block_pairs, prefix_lengths))
        update = jnp.dot(attended.reshape(ROWS * BLOCK, HEADS * HEAD), layer_rows, preferred_element_type=jnp.float32)
        update = update.reshape(ROWS, BLOCK, D) * (HEADS * HEAD) ** (-0.5)
        current_state = revise(current_state, update, position_picks[step_index], mask_vector)
    return (current_state, new_weight, new_first, new_second)
```

```python
import jax
import jax.numpy as jnp
from jax import lax
from jax.sharding import Mesh, PartitionSpec as P

HEADS = 64
HEAD = 128
STEPS = 2

BETA_ONE = 0.9
BETA_TWO = 0.95
ADAM_EPS = 1e-08
LEARN_RATE = 0.5
DECAY_RATE = 0.1
STEP_COUNT = 50
NORM_EPS = 1e-06

RD = ("role", "dp")
TENSOR = ("x", "y", "core")
EVERY = RD + TENSOR


def rotate(block, axis, shift):
    count = lax.axis_size(axis)
    return lax.ppermute(block, axis, [(low, (low + shift) % count) for low in range(count)])


def pick(blocks, index):
    return lax.dynamic_index_in_dim(blocks, index, 0, keepdims=False)


def pair_order(own, other, index, axis):
    return jnp.where(index == 0, jnp.stack([own, other], axis), jnp.stack([other, own], axis))


def adam_update(gradient, master_weight, first_moment, second_moment):
    first_new = BETA_ONE * first_moment + (1.0 - BETA_ONE) * gradient
    second_new = BETA_TWO * second_moment + (1.0 - BETA_TWO) * gradient * gradient
    first_hat = first_new / (1.0 - BETA_ONE**STEP_COUNT)
    second_hat = second_new / (1.0 - BETA_TWO**STEP_COUNT)
    weight_new = master_weight - LEARN_RATE * (
        first_hat / (jnp.sqrt(second_hat) + ADAM_EPS) + DECAY_RATE * master_weight
    )
    return (weight_new, first_new, second_new)


def gather_features(part):
    iy, ix, ic = lax.axis_index("y"), lax.axis_index("x"), lax.axis_index("core")
    rows = pair_order(part, rotate(part, "y", 1), iy, 0)
    ahead, back, across = rotate(rows, "x", 1), rotate(rows, "x", -1), rotate(rows, "x", 2)
    square = jnp.zeros((4,) + rows.shape, rows.dtype)
    square = lax.dynamic_update_index_in_dim(square, rows, ix, 0)
    square = lax.dynamic_update_index_in_dim(square, ahead, (ix + 3) % 4, 0)
    square = lax.dynamic_update_index_in_dim(square, back, (ix + 1) % 4, 0)
    square = lax.dynamic_update_index_in_dim(square, across, (ix + 2) % 4, 0)
    whole = pair_order(square, rotate(square, "core", 1), ic, 2)
    return whole.reshape(-1, part.shape[-1])


def scatter_sum(parts):
    iy, ix, ic = lax.axis_index("y"), lax.axis_index("x"), lax.axis_index("core")
    bf16, f32 = jnp.bfloat16, jnp.float32
    away = lax.dynamic_index_in_dim(parts, 1 - ic, 2, keepdims=False).astype(bf16)
    near = lax.dynamic_index_in_dim(parts, ic, 2, keepdims=False)
    sums = near + rotate(away, "core", 1).astype(f32)
    sent = sums.astype(bf16)
    ahead = rotate(pick(sent, (ix + 1) % 4), "x", 1)
    back = rotate(pick(sent, (ix + 3) % 4), "x", -1)
    across = rotate(pick(sent, (ix + 2) % 4), "x", 2)
    sums = pick(sums, ix) + ahead.astype(f32) + back.astype(f32) + across.astype(f32)
    return pick(sums, iy) + rotate(pick(sums, 1 - iy).astype(bf16), "y", 1).astype(f32)


def normalize(state, norm_gain):
    values = state.astype(jnp.float32)
    mean_square = jnp.mean(values * values, axis=0, keepdims=True)
    return (values * lax.rsqrt(mean_square + NORM_EPS) * norm_gain[:, None]).astype(jnp.bfloat16)


def revise(current_state, update, pick_codes, mask_values):
    values = current_state.astype(jnp.float32)
    masked = jnp.broadcast_to(mask_values.astype(jnp.float32)[:, None], values.shape)
    return jnp.where(
        pick_codes == 1, values + update, jnp.where(pick_codes == 2, masked, values)
    ).astype(jnp.bfloat16)


def attend(queries, cache_keys, cache_values, block_keys, block_values, prefix_lengths):
    score_scale = HEAD ** (-0.5)
    prefix_len = cache_keys.shape[1]
    prefix_scores = (
        jnp.einsum("rbgh,rph->rgbp", queries, cache_keys, preferred_element_type=jnp.float32)
        * score_scale
    )
    valid_keys = jnp.arange(prefix_len, dtype=jnp.int32)[None, :] < prefix_lengths[:, None]
    prefix_scores = jnp.where(valid_keys[:, None, None, :], prefix_scores, -jnp.inf)
    block_scores = (
        jnp.einsum("rbgh,rch->rgbc", queries, block_keys, preferred_element_type=jnp.float32)
        * score_scale
    )
    score_top = jnp.maximum(jnp.max(prefix_scores, axis=-1), jnp.max(block_scores, axis=-1))[
        ..., None
    ]
    prefix_exp = jnp.exp(prefix_scores - score_top)
    block_exp = jnp.exp(block_scores - score_top)
    denom_sum = (jnp.sum(prefix_exp, axis=-1) + jnp.sum(block_exp, axis=-1))[..., None]
    prefix_probs = (prefix_exp / denom_sum).astype(jnp.bfloat16)
    block_probs = (block_exp / denom_sum).astype(jnp.bfloat16)
    attended = jnp.einsum(
        "rgbp,rph->rbgh", prefix_probs, cache_values, preferred_element_type=jnp.float32
    )
    attended = attended + jnp.einsum(
        "rgbc,rch->rbgh", block_probs, block_values, preferred_element_type=jnp.float32
    )
    return attended.astype(jnp.bfloat16).reshape(queries.shape[0] * queries.shape[1], -1)


def on_device(
    learner_inputs,
    learner_cotangent,
    master_weight,
    first_moment,
    second_moment,
    query_weight,
    keyval_weight,
    prefix_cache,
    block_states,
    norm_gain,
    mask_vector,
    prefix_lengths,
    position_picks,
):
    bf16, f32 = jnp.bfloat16, jnp.float32
    role, core = lax.axis_index("role"), lax.axis_index("core")
    rows, block_len, part = block_states.shape
    tokens = rows * block_len
    depth = learner_inputs.shape[1]
    out_scale = (HEADS * HEAD) ** (-0.5)

    cache_other = rotate(prefix_cache, "core", 1)
    cache_keys = jnp.where(core == 0, prefix_cache, cache_other)
    cache_values = jnp.where(core == 0, cache_other, prefix_cache)
    mask_part = lax.dynamic_slice_in_dim(mask_vector, lax.axis_index(TENSOR) * part, part, 0)

    def attended_of(state):
        normed = normalize(gather_features(state), norm_gain)
        own_half = lax.dot_general(
            normed, keyval_weight, (((0,), (0,)), ((), ())), preferred_element_type=f32
        ).astype(bf16)
        other_half = rotate(own_half, "core", 1)
        queries = lax.dot_general(
            normed, query_weight, (((0,), (0,)), ((), ())), preferred_element_type=f32
        ).astype(bf16)
        block_keys = jnp.where(core == 0, own_half, other_half).reshape(rows, block_len, HEAD)
        block_values = jnp.where(core == 0, other_half, own_half).reshape(rows, block_len, HEAD)
        return attend(
            queries.reshape(rows, block_len, -1, HEAD),
            cache_keys,
            cache_values,
            block_keys,
            block_values,
            prefix_lengths,
        )

    state = block_states.reshape(tokens, part).T
    attended = attended_of(state)
    both = pair_order(attended, rotate(attended, "role", 1), role, 0)
    attended_all = lax.all_gather(both, "dp", axis=0)

    cotangent = lax.all_gather(learner_cotangent, TENSOR, axis=1, tiled=True)
    terms = lax.dot_general(
        cotangent, learner_inputs, (((0,), (0,)), ((), ())), preferred_element_type=f32
    ).astype(bf16)
    terms = terms.reshape(2, 8, part, depth).transpose(1, 0, 2, 3)
    halves = lax.psum_scatter(terms, "dp", scatter_dimension=0, tiled=False)
    gradient = pick(halves, role).astype(f32) + rotate(pick(halves, 1 - role), "role", 1).astype(f32)
    new_weight, new_first, new_second = adam_update(
        gradient, master_weight.T, first_moment.T, second_moment.T
    )
    weight_part = new_weight.astype(bf16)

    weight_both = pair_order(weight_part, rotate(weight_part, "role", 1), role, 0)
    weight_all = lax.all_gather(weight_both, "dp", axis=0)

    partial = jnp.einsum("ck,drtk->rdct", weight_part, attended_all, preferred_element_type=f32)
    update = scatter_sum(partial.reshape(4, 2, 2, part, tokens))
    swap = [(a * 16 + b, b * 16 + a) for a in range(16) for b in range(16)]
    update = lax.ppermute(update.astype(bf16), EVERY, swap).astype(f32) * out_scale
    picks = position_picks.reshape(STEPS, 1, tokens)
    state = revise(state, update, picks[0], mask_part)

    attended = attended_of(state)
    partial = jnp.einsum("drck,tk->rdct", weight_all, attended, preferred_element_type=f32)
    update = scatter_sum(partial.reshape(4, 2, 2, part, tokens)) * out_scale
    state = revise(state, update, picks[1], mask_part)
    return (state.T.reshape(rows, block_len, part), new_weight.T, new_first.T, new_second.T)


def solution(mesh):
    fine = Mesh(mesh.devices.reshape(2, 8, 4, 2, 2), EVERY)
    weights = P(TENSOR, RD)
    return jax.shard_map(
        on_device,
        mesh=fine,
        in_specs=(
            P(RD, TENSOR),
            P(RD, TENSOR),
            weights,
            weights,
            weights,
            P(None, TENSOR),
            P(None, TENSOR),
            P(RD, None, TENSOR),
            P(RD, None, TENSOR),
            P(),
            P(),
            P(RD),
            P(None, RD, None),
        ),
        out_specs=(P(RD, None, TENSOR), weights, weights, weights),
        check_vma=False,
    )
```

```python
import jax
import jax.numpy as jnp
from jax import lax
from jax.experimental import pallas as pl
from jax.experimental.pallas import tpu as pltpu
from jax.sharding import Mesh, PartitionSpec as P

HEADS = 64
HEAD = 128
STEPS = 2

BETA_ONE = 0.9
BETA_TWO = 0.95
ADAM_EPS = 1e-08
LEARN_RATE = 0.5
DECAY_RATE = 0.1
STEP_COUNT = 50
NORM_EPS = 1e-06

RD = ("role", "dp")
TENSOR = ("x", "y", "core")
EVERY = RD + TENSOR


def rotate(block, axis, shift):
    count = lax.axis_size(axis)
    return lax.ppermute(block, axis, [(low, (low + shift) % count) for low in range(count)])


def pick(blocks, index):
    return lax.dynamic_index_in_dim(blocks, index, 0, keepdims=False)


def pair_order(own, other, index, axis):
    return jnp.where(index == 0, jnp.stack([own, other], axis), jnp.stack([other, own], axis))


def adam_update(gradient, master_weight, first_moment, second_moment):
    first_new = BETA_ONE * first_moment + (1.0 - BETA_ONE) * gradient
    second_new = BETA_TWO * second_moment + (1.0 - BETA_TWO) * gradient * gradient
    first_hat = first_new / (1.0 - BETA_ONE**STEP_COUNT)
    second_hat = second_new / (1.0 - BETA_TWO**STEP_COUNT)
    weight_new = master_weight - LEARN_RATE * (
        first_hat / (jnp.sqrt(second_hat) + ADAM_EPS) + DECAY_RATE * master_weight
    )
    return (weight_new, first_new, second_new)


def gather_features(part):
    iy, ix, ic = lax.axis_index("y"), lax.axis_index("x"), lax.axis_index("core")
    rows = pair_order(part, rotate(part, "y", 1), iy, 0)
    ahead, back, across = rotate(rows, "x", 1), rotate(rows, "x", -1), rotate(rows, "x", 2)
    square = jnp.zeros((4,) + rows.shape, rows.dtype)
    square = lax.dynamic_update_index_in_dim(square, rows, ix, 0)
    square = lax.dynamic_update_index_in_dim(square, ahead, (ix + 3) % 4, 0)
    square = lax.dynamic_update_index_in_dim(square, back, (ix + 1) % 4, 0)
    square = lax.dynamic_update_index_in_dim(square, across, (ix + 2) % 4, 0)
    whole = pair_order(square, rotate(square, "core", 1), ic, 2)
    return whole.reshape(-1, part.shape[-1])


def swap_cores(block, flip_role):
    route = []
    for role in range(2):
        for dp in range(8):
            for core in range(2):
                low = dp % 2
                source = (role * 8 + dp) * 2 + core
                target_role = 1 - role if flip_role else role
                target = (target_role * 8 + dp - low + core) * 2 + low
                route.append((source, target))
    return lax.ppermute(block, ("role", "dp", "core"), route)


def gather_ring(block):
    me = lax.axis_index("dp")
    whole = jnp.zeros((8,) + block.shape, block.dtype)
    whole = lax.dynamic_update_index_in_dim(whole, block, me, 0)
    up = down = block
    for step in range(1, 5):
        up = rotate(up, "dp", 1)
        whole = lax.dynamic_update_index_in_dim(whole, up, (me + 8 - step) % 8, 0)
        if step < 4:
            down = rotate(down, "dp", -1)
            whole = lax.dynamic_update_index_in_dim(whole, down, (me + step) % 8, 0)
    return whole


def scatter_sum(parts):
    blocks = lax.all_to_all(parts, ("x", "y"), 0, 0, tiled=True)
    return jnp.sum(blocks.astype(jnp.float32), axis=0)


def gradient_kernel(cotangent_ref, inputs_ref, out_ref):
    out_ref[0, 0] = jnp.dot(
        cotangent_ref[...], inputs_ref[...], preferred_element_type=jnp.float32
    ).astype(out_ref.dtype)


def gradient_terms(cotangent, inputs):
    tokens, depth = inputs.shape
    part = cotangent.shape[0] // 16
    return pl.pallas_call(
        gradient_kernel,
        grid=(16,),
        in_specs=[
            pl.BlockSpec((part, tokens), lambda j: (j, 0)),
            pl.BlockSpec((tokens, depth), lambda j: (0, 0)),
        ],
        out_specs=pl.BlockSpec((1, 1, part, depth), lambda j: (j % 8, j // 8, 0, 0)),
        out_shape=jax.ShapeDtypeStruct((8, 2, part, depth), jnp.bfloat16),
        compiler_params=pltpu.CompilerParams(vmem_limit_bytes=32 * 1024 * 1024),
        cost_estimate=pl.CostEstimate(
            flops=2 * 16 * part * tokens * depth, bytes_accessed=17_000_000, transcendentals=0
        ),
    )(cotangent, inputs)


def project_kernel(weight_ref, tokens_ref, out_ref):
    dims = (((1,), (1,)), ((), ()))
    total = lax.dot_general(
        weight_ref[0, 0, 0], tokens_ref[0, 0, 0], dims, preferred_element_type=jnp.float32
    )
    total += lax.dot_general(
        weight_ref[0, 1, 0], tokens_ref[0, 1, 0], dims, preferred_element_type=jnp.float32
    )
    out_ref[0, 0] = total.astype(out_ref.dtype)


def project(weight, attended):
    part, depth = weight.shape[3:]
    tokens = attended.shape[3]

    def spec(array):
        several = array.shape[0] > 1
        return pl.BlockSpec(
            (1, 2, 1) + array.shape[3:],
            (lambda r, k: (k, 0, r, 0, 0)) if several else (lambda r, k: (0, 0, 0, 0, 0)),
        )

    out = pl.pallas_call(
        project_kernel,
        grid=(2, 4),
        in_specs=[spec(weight), spec(attended)],
        out_specs=pl.BlockSpec((1, 1, part, tokens), lambda r, k: (r, k, 0, 0)),
        out_shape=jax.ShapeDtypeStruct((2, 4, part, tokens), jnp.bfloat16),
        compiler_params=pltpu.CompilerParams(vmem_limit_bytes=32 * 1024 * 1024),
        cost_estimate=pl.CostEstimate(
            flops=32 * part * depth * tokens, bytes_accessed=6_000_000, transcendentals=0
        ),
    )(weight, attended)
    return out.reshape(8, part, tokens)


def normalize(state, norm_gain):
    values = state.astype(jnp.float32)
    mean_square = jnp.mean(values * values, axis=0, keepdims=True)
    return (values * lax.rsqrt(mean_square + NORM_EPS) * norm_gain[:, None]).astype(jnp.bfloat16)


def revise(current_state, update, pick_codes, mask_values):
    values = current_state.astype(jnp.float32)
    masked = jnp.broadcast_to(mask_values.astype(jnp.float32)[:, None], values.shape)
    return jnp.where(
        pick_codes == 1, values + update, jnp.where(pick_codes == 2, masked, values)
    ).astype(jnp.bfloat16)


def attend(queries, cache_keys, cache_values, block_keys, block_values, prefix_lengths):
    score_scale = HEAD ** (-0.5)
    prefix_len = cache_keys.shape[1]
    prefix_scores = (
        jnp.einsum("rbgh,rph->rgbp", queries, cache_keys, preferred_element_type=jnp.float32)
        * score_scale
    )
    valid_keys = jnp.arange(prefix_len, dtype=jnp.int32)[None, :] < prefix_lengths[:, None]
    prefix_scores = jnp.where(valid_keys[:, None, None, :], prefix_scores, -jnp.inf)
    block_scores = (
        jnp.einsum("rbgh,rch->rgbc", queries, block_keys, preferred_element_type=jnp.float32)
        * score_scale
    )
    score_top = jnp.maximum(jnp.max(prefix_scores, axis=-1), jnp.max(block_scores, axis=-1))[
        ..., None
    ]
    prefix_exp = jnp.exp(prefix_scores - score_top)
    block_exp = jnp.exp(block_scores - score_top)
    denom_sum = (jnp.sum(prefix_exp, axis=-1) + jnp.sum(block_exp, axis=-1))[..., None]
    prefix_probs = (prefix_exp / denom_sum).astype(jnp.bfloat16)
    block_probs = (block_exp / denom_sum).astype(jnp.bfloat16)
    attended = jnp.einsum(
        "rgbp,rph->rbgh", prefix_probs, cache_values, preferred_element_type=jnp.float32
    )
    attended = attended + jnp.einsum(
        "rgbc,rch->rbgh", block_probs, block_values, preferred_element_type=jnp.float32
    )
    return attended.astype(jnp.bfloat16).reshape(queries.shape[0] * queries.shape[1], -1)


def on_device(
    learner_inputs,
    learner_cotangent,
    master_weight,
    first_moment,
    second_moment,
    query_weight,
    keyval_weight,
    prefix_cache,
    block_states,
    norm_gain,
    mask_vector,
    prefix_lengths,
    position_picks,
):
    bf16, f32 = jnp.bfloat16, jnp.float32
    role, core = lax.axis_index("role"), lax.axis_index("core")
    rows, block_len, part = block_states.shape
    tokens = rows * block_len
    depth = learner_inputs.shape[1]
    out_scale = (HEADS * HEAD) ** (-0.5)

    cache_other = rotate(prefix_cache, "core", 1)
    cache_keys = jnp.where(core == 0, prefix_cache, cache_other)
    cache_values = jnp.where(core == 0, cache_other, prefix_cache)
    mask_part = lax.dynamic_slice_in_dim(mask_vector, lax.axis_index(TENSOR) * part, part, 0)

    def attended_of(state):
        normed = normalize(gather_features(state), norm_gain)
        own_half = lax.dot_general(
            normed, keyval_weight, (((0,), (0,)), ((), ())), preferred_element_type=f32
        ).astype(bf16)
        other_half = rotate(own_half, "core", 1)
        queries = lax.dot_general(
            normed, query_weight, (((0,), (0,)), ((), ())), preferred_element_type=f32
        ).astype(bf16)
        block_keys = jnp.where(core == 0, own_half, other_half).reshape(rows, block_len, HEAD)
        block_values = jnp.where(core == 0, other_half, own_half).reshape(rows, block_len, HEAD)
        return attend(
            queries.reshape(rows, block_len, -1, HEAD),
            cache_keys,
            cache_values,
            block_keys,
            block_values,
            prefix_lengths,
        )

    cotangent = lax.all_gather(learner_cotangent, TENSOR, axis=1, tiled=True)
    state = block_states.reshape(tokens, part).T
    attended = attended_of(state)
    both = pair_order(swap_cores(attended, False), swap_cores(attended, True), role, 0)
    attended_all = gather_ring(both)
    cotangent, attended_all = lax.optimization_barrier((cotangent, attended_all))

    terms = gradient_terms(cotangent.T, learner_inputs)
    halves = lax.psum_scatter(terms, "dp", scatter_dimension=0, tiled=False)
    gradient = pick(halves, role).astype(f32) + rotate(pick(halves, 1 - role), "role", 1).astype(f32)
    new_weight, new_first, new_second = adam_update(
        gradient, master_weight.T, first_moment.T, second_moment.T
    )
    weight_part = new_weight.astype(bf16)
    weight_pair = pair_order(weight_part, rotate(weight_part, "core", 1), core, 0)

    weight_both = pair_order(swap_cores(weight_part, False), swap_cores(weight_part, True), role, 0)
    weight_all = lax.all_gather(weight_both, "dp", axis=0)

    partial = project(
        weight_pair.reshape(1, 2, 1, part, depth), attended_all.reshape(4, 2, 2, tokens, depth)
    )
    update = scatter_sum(partial)
    swap = [(a * 16 + b, b * 16 + a) for a in range(16) for b in range(16)]
    update = lax.ppermute(update.astype(bf16), EVERY, swap).astype(f32) * out_scale
    picks = position_picks.reshape(STEPS, 1, tokens)
    state = revise(state, update, picks[0], mask_part)

    attended = attended_of(state)
    attended_pair = pair_order(attended, rotate(attended, "core", 1), core, 0)
    partial = project(
        weight_all.reshape(4, 2, 2, part, depth), attended_pair.reshape(1, 2, 1, tokens, depth)
    )
    update = scatter_sum(partial) * out_scale
    state = revise(state, update, picks[1], mask_part)
    return (state.T.reshape(rows, block_len, part), new_weight.T, new_first.T, new_second.T)


def solution(mesh):
    fine = Mesh(mesh.devices.reshape(2, 8, 4, 2, 2), EVERY)
    weights = P(TENSOR, RD)
    return jax.shard_map(
        on_device,
        mesh=fine,
        in_specs=(
            P(RD, TENSOR),
            P(RD, TENSOR),
            weights,
            weights,
            weights,
            P(None, TENSOR),
            P(None, TENSOR),
            P(RD, None, TENSOR),
            P(RD, None, TENSOR),
            P(),
            P(),
            P(RD),
            P(None, RD, None),
        ),
        out_specs=(P(RD, None, TENSOR), weights, weights, weights),
        check_vma=False,
    )
```

```python
import jax
import jax.numpy as jnp
from jax import lax
from jax.experimental import pallas as pl
from jax.experimental.pallas import tpu as pltpu
from jax.sharding import Mesh, PartitionSpec as P

HEADS = 64
HEAD = 128
STEPS = 2

BETA_ONE = 0.9
BETA_TWO = 0.95
ADAM_EPS = 1e-08
LEARN_RATE = 0.5
DECAY_RATE = 0.1
STEP_COUNT = 50
NORM_EPS = 1e-06

RD = ("role", "dp")
TENSOR = ("x", "y", "core")
EVERY = RD + TENSOR


def rotate(block, axis, shift):
    count = lax.axis_size(axis)
    return lax.ppermute(block, axis, [(low, (low + shift) % count) for low in range(count)])


def pick(blocks, index):
    return lax.dynamic_index_in_dim(blocks, index, 0, keepdims=False)


def pair_order(own, other, index, axis):
    return jnp.where(index == 0, jnp.stack([own, other], axis), jnp.stack([other, own], axis))


def adam_update(gradient, master_weight, first_moment, second_moment):
    first_new = BETA_ONE * first_moment + (1.0 - BETA_ONE) * gradient
    second_new = BETA_TWO * second_moment + (1.0 - BETA_TWO) * gradient * gradient
    first_hat = first_new / (1.0 - BETA_ONE**STEP_COUNT)
    second_hat = second_new / (1.0 - BETA_TWO**STEP_COUNT)
    weight_new = master_weight - LEARN_RATE * (
        first_hat / (jnp.sqrt(second_hat) + ADAM_EPS) + DECAY_RATE * master_weight
    )
    return (weight_new, first_new, second_new)


def gather_features(part, beside=None):
    iy, ix, ic = lax.axis_index("y"), lax.axis_index("x"), lax.axis_index("core")
    rows = pair_order(part, rotate(part, "y", 1), iy, 0)
    ahead, back, across = rotate(rows, "x", 1), rotate(rows, "x", -1), rotate(rows, "x", 2)
    square = jnp.zeros((4,) + rows.shape, rows.dtype)
    square = lax.dynamic_update_index_in_dim(square, rows, ix, 0)
    square = lax.dynamic_update_index_in_dim(square, ahead, (ix + 3) % 4, 0)
    square = lax.dynamic_update_index_in_dim(square, back, (ix + 1) % 4, 0)
    square = lax.dynamic_update_index_in_dim(square, across, (ix + 2) % 4, 0)
    square, beside = lax.optimization_barrier((square, beside))
    whole = pair_order(square, rotate(square, "core", 1), ic, 2)
    return whole.reshape(-1, part.shape[-1]), beside


def swap_cores(block, flip_role=False):
    route = []
    for role in range(2):
        for dp in range(8):
            for core in range(2):
                low = dp % 2
                source = (role * 8 + dp) * 2 + core
                target_role = 1 - role if flip_role else role
                target = (target_role * 8 + dp - low + core) * 2 + low
                route.append((source, target))
    return lax.ppermute(block, ("role", "dp", "core"), route)


def gather_ring(block, before):
    me = lax.axis_index("dp")
    up, down = [block], [block]
    for step in range(3):
        up.append(rotate(up[-1], "dp", 1))
        down.append(rotate(down[-1], "dp", -1))
    before, up, down = lax.optimization_barrier((before, up, down))
    up.append(rotate(up[-1], "dp", 1))
    whole = jnp.zeros((8,) + block.shape, block.dtype)
    for step in range(5):
        whole = lax.dynamic_update_index_in_dim(whole, up[step], (me + 8 - step) % 8, 0)
    for step in range(1, 4):
        whole = lax.dynamic_update_index_in_dim(whole, down[step], (me + step) % 8, 0)
    return whole, before


def scatter_sum(parts):
    blocks = lax.all_to_all(parts, ("x", "y"), 0, 0, tiled=True)
    return jnp.sum(blocks.astype(jnp.float32), axis=0)


def gradient_kernel(cotangent_ref, inputs_ref, out_ref):
    out_ref[0, 0] = jnp.dot(
        cotangent_ref[...], inputs_ref[...], preferred_element_type=jnp.float32
    ).astype(out_ref.dtype)


def gradient_terms(cotangent, inputs):
    tokens, depth = inputs.shape
    part = cotangent.shape[0] // 16
    return pl.pallas_call(
        gradient_kernel,
        grid=(16,),
        in_specs=[
            pl.BlockSpec((part, tokens), lambda j: (j, 0)),
            pl.BlockSpec((tokens, depth), lambda j: (0, 0)),
        ],
        out_specs=pl.BlockSpec((1, 1, part, depth), lambda j: (j % 8, j // 8, 0, 0)),
        out_shape=jax.ShapeDtypeStruct((8, 2, part, depth), jnp.bfloat16),
        compiler_params=pltpu.CompilerParams(vmem_limit_bytes=60 * 1024 * 1024),
        cost_estimate=pl.CostEstimate(
            flops=2 * 16 * part * tokens * depth, bytes_accessed=17_000_000, transcendentals=0
        ),
    )(cotangent, inputs)


def project_kernel(weight_ref, tokens_ref, out_ref):
    dims = (((1,), (1,)), ((), ()))
    total = lax.dot_general(
        weight_ref[0, 0, 0], tokens_ref[0, 0, 0], dims, preferred_element_type=jnp.float32
    )
    total += lax.dot_general(
        weight_ref[0, 1, 0], tokens_ref[0, 1, 0], dims, preferred_element_type=jnp.float32
    )
    out_ref[0, 0] = total.astype(out_ref.dtype)


def project(weight, attended):
    part, depth = weight.shape[3:]
    tokens = attended.shape[3]

    def spec(array):
        pairs, _, roles = array.shape[:3]
        return pl.BlockSpec(
            (1, 2, 1) + array.shape[3:],
            lambda r, k: (k if pairs > 1 else 0, 0, r if roles > 1 else 0, 0, 0),
        )

    out = pl.pallas_call(
        project_kernel,
        grid=(2, 4),
        in_specs=[spec(weight), spec(attended)],
        out_specs=pl.BlockSpec((1, 1, part, tokens), lambda r, k: (r, k, 0, 0)),
        out_shape=jax.ShapeDtypeStruct((2, 4, part, tokens), jnp.bfloat16),
        compiler_params=pltpu.CompilerParams(vmem_limit_bytes=32 * 1024 * 1024),
        cost_estimate=pl.CostEstimate(
            flops=32 * part * depth * tokens, bytes_accessed=6_000_000, transcendentals=0
        ),
    )(weight, attended)
    return out.reshape(8, part, tokens)


def normalize(state, norm_gain):
    values = state.astype(jnp.float32)
    mean_square = jnp.mean(values * values, axis=0, keepdims=True)
    return (values * lax.rsqrt(mean_square + NORM_EPS) * norm_gain[:, None]).astype(jnp.bfloat16)


def revise(current_state, update, pick_codes, mask_values):
    values = current_state.astype(jnp.float32)
    masked = jnp.broadcast_to(mask_values.astype(jnp.float32)[:, None], values.shape)
    return jnp.where(
        pick_codes == 1, values + update, jnp.where(pick_codes == 2, masked, values)
    ).astype(jnp.bfloat16)


def attend(queries, cache_keys, cache_values, block_keys, block_values, prefix_lengths):
    score_scale = HEAD ** (-0.5)
    prefix_len = cache_keys.shape[1]
    prefix_scores = (
        jnp.einsum("rbgh,rph->rgbp", queries, cache_keys, preferred_element_type=jnp.float32)
        * score_scale
    )
    valid_keys = jnp.arange(prefix_len, dtype=jnp.int32)[None, :] < prefix_lengths[:, None]
    prefix_scores = jnp.where(valid_keys[:, None, None, :], prefix_scores, -jnp.inf)
    block_scores = (
        jnp.einsum("rbgh,rch->rgbc", queries, block_keys, preferred_element_type=jnp.float32)
        * score_scale
    )
    score_top = jnp.maximum(jnp.max(prefix_scores, axis=-1), jnp.max(block_scores, axis=-1))[
        ..., None
    ]
    prefix_exp = jnp.exp(prefix_scores - score_top)
    block_exp = jnp.exp(block_scores - score_top)
    denom_sum = (jnp.sum(prefix_exp, axis=-1) + jnp.sum(block_exp, axis=-1))[..., None]
    prefix_probs = (prefix_exp / denom_sum).astype(jnp.bfloat16)
    block_probs = (block_exp / denom_sum).astype(jnp.bfloat16)
    attended = jnp.einsum(
        "rgbp,rph->rbgh", prefix_probs, cache_values, preferred_element_type=jnp.float32
    )
    attended = attended + jnp.einsum(
        "rgbc,rch->rbgh", block_probs, block_values, preferred_element_type=jnp.float32
    )
    return attended.astype(jnp.bfloat16).reshape(queries.shape[0] * queries.shape[1], -1)


def on_device(
    learner_inputs,
    learner_cotangent,
    master_weight,
    first_moment,
    second_moment,
    query_weight,
    keyval_weight,
    prefix_cache,
    block_states,
    norm_gain,
    mask_vector,
    prefix_lengths,
    position_picks,
):
    bf16, f32 = jnp.bfloat16, jnp.float32
    role, core = lax.axis_index("role"), lax.axis_index("core")
    rows, block_len, part = block_states.shape
    tokens = rows * block_len
    depth = learner_inputs.shape[1]
    out_scale = (HEADS * HEAD) ** (-0.5)

    cache_other = rotate(prefix_cache, "core", 1)
    cache_keys = jnp.where(core == 0, prefix_cache, cache_other)
    cache_values = jnp.where(core == 0, cache_other, prefix_cache)
    mask_part = lax.dynamic_slice_in_dim(mask_vector, lax.axis_index(TENSOR) * part, part, 0)

    def attended_of(state, beside=None):
        whole, beside = gather_features(state, beside)
        normed = normalize(whole, norm_gain)
        own_half = lax.dot_general(
            normed, keyval_weight, (((0,), (0,)), ((), ())), preferred_element_type=f32
        ).astype(bf16)
        other_half = rotate(own_half, "core", 1)
        queries = lax.dot_general(
            normed, query_weight, (((0,), (0,)), ((), ())), preferred_element_type=f32
        ).astype(bf16)
        block_keys = jnp.where(core == 0, own_half, other_half).reshape(rows, block_len, HEAD)
        block_values = jnp.where(core == 0, other_half, own_half).reshape(rows, block_len, HEAD)
        attended = attend(
            queries.reshape(rows, block_len, -1, HEAD),
            cache_keys,
            cache_values,
            block_keys,
            block_values,
            prefix_lengths,
        )
        return attended, beside

    cotangent = lax.all_gather(learner_cotangent, TENSOR, axis=1, tiled=True)
    state = block_states.reshape(tokens, part).T
    attended, _ = attended_of(state)
    both = pair_order(swap_cores(attended, False), swap_cores(attended, True), role, 0)
    attended_all, cotangent = gather_ring(both, cotangent)

    terms = gradient_terms(cotangent.T, learner_inputs)
    halves = lax.psum_scatter(terms, "dp", scatter_dimension=0, tiled=False)
    gradient = pick(halves, role).astype(f32) + rotate(pick(halves, 1 - role), "role", 1).astype(f32)
    new_weight, new_first, new_second = adam_update(
        gradient, master_weight.T, first_moment.T, second_moment.T
    )
    weight_part = new_weight.astype(bf16)
    weight_pair = pair_order(weight_part, rotate(weight_part, "core", 1), core, 0)

    partial = project(
        weight_pair.reshape(1, 2, 1, part, depth), attended_all.reshape(4, 2, 2, tokens, depth)
    )
    weight_half, partial = lax.optimization_barrier((swap_cores(weight_part), partial))
    weight_all = lax.all_gather(weight_half, "dp", axis=0)
    update = scatter_sum(partial)
    swap = [(a * 16 + b, b * 16 + a) for a in range(16) for b in range(16)]
    update = lax.ppermute(update.astype(bf16), EVERY, swap).astype(f32) * out_scale
    picks = position_picks.reshape(STEPS, 1, tokens)
    state = revise(state, update, picks[0], mask_part)

    attended, weight_all = attended_of(state, weight_all)
    attended_pair = pair_order(attended, rotate(attended, "core", 1), core, 0)
    route = [(r * 2 + c, (1 - r) * 2 + 1 - c) for r in range(2) for c in range(2)]
    far = lax.ppermute(attended, ("role", "core"), route)
    far_pair = pair_order(rotate(attended, "role", 1), far, core, 0)
    attended_four = pair_order(attended_pair, far_pair, role, 1)
    partial = project(weight_all.reshape(4, 2, 1, part, depth), attended_four[None])
    update = scatter_sum(partial).astype(bf16)
    route = [(r * 4 + x, (x // 2) * 4 + r * 2 + x % 2) for r in range(2) for x in range(4)]
    update = lax.ppermute(update, ("role", "x"), route).astype(f32) * out_scale
    state = revise(state, update, picks[1], mask_part)
    return (state.T.reshape(rows, block_len, part), new_weight.T, new_first.T, new_second.T)


def solution(mesh):
    fine = Mesh(mesh.devices.reshape(2, 8, 4, 2, 2), EVERY)
    weights = P(TENSOR, RD)
    return jax.shard_map(
        on_device,
        mesh=fine,
        in_specs=(
            P(RD, TENSOR),
            P(RD, TENSOR),
            weights,
            weights,
            weights,
            P(None, TENSOR),
            P(None, TENSOR),
            P(RD, None, TENSOR),
            P(RD, None, TENSOR),
            P(),
            P(),
            P(RD),
            P(None, RD, None),
        ),
        out_specs=(P(RD, None, TENSOR), weights, weights, weights),
        check_vma=False,
    )
```

```python
import jax
import jax.numpy as jnp
from jax import lax
from jax.experimental import pallas as pl
from jax.experimental.pallas import tpu as pltpu
from jax.sharding import Mesh, PartitionSpec as P

HEADS = 64
HEAD = 128
STEPS = 2

BETA_ONE = 0.9
BETA_TWO = 0.95
ADAM_EPS = 1e-08
LEARN_RATE = 0.5
DECAY_RATE = 0.1
STEP_COUNT = 50
NORM_EPS = 1e-06

RD = ("role", "dp")
X = ("x1", "x0")
TENSOR = X + ("y", "core")
EVERY = RD + TENSOR


def rotate(block, axis, shift):
    count = 4 if axis == X else lax.axis_size(axis)
    return lax.ppermute(block, axis, [(low, (low + shift) % count) for low in range(count)])


def pick(blocks, index):
    return lax.dynamic_index_in_dim(blocks, index, 0, keepdims=False)


def pair_order(own, other, index, axis):
    return jnp.where(index == 0, jnp.stack([own, other], axis), jnp.stack([other, own], axis))


def adam_update(gradient, master_weight, first_moment, second_moment):
    first_new = BETA_ONE * first_moment + (1.0 - BETA_ONE) * gradient
    second_new = BETA_TWO * second_moment + (1.0 - BETA_TWO) * gradient * gradient
    first_hat = first_new / (1.0 - BETA_ONE**STEP_COUNT)
    second_hat = second_new / (1.0 - BETA_TWO**STEP_COUNT)
    weight_new = master_weight - LEARN_RATE * (
        first_hat / (jnp.sqrt(second_hat) + ADAM_EPS) + DECAY_RATE * master_weight
    )
    return (weight_new, first_new, second_new)


def gather_features(part, shift_x, shift_y, beside=None):
    iy, ix, ic = lax.axis_index("y"), lax.axis_index(X), lax.axis_index("core")
    rows = pair_order(part, rotate(part, "y", 1), iy ^ shift_y, 0)
    ahead, back, across = rotate(rows, X, 1), rotate(rows, X, -1), rotate(rows, X, 2)
    square = jnp.zeros((4,) + rows.shape, rows.dtype)
    square = lax.dynamic_update_index_in_dim(square, rows, ix ^ shift_x, 0)
    square = lax.dynamic_update_index_in_dim(square, ahead, ((ix + 3) % 4) ^ shift_x, 0)
    square = lax.dynamic_update_index_in_dim(square, back, ((ix + 1) % 4) ^ shift_x, 0)
    square = lax.dynamic_update_index_in_dim(square, across, ((ix + 2) % 4) ^ shift_x, 0)
    square, beside = lax.optimization_barrier((square, beside))
    whole = pair_order(square, rotate(square, "core", 1), ic, 2)
    return whole.reshape((16,) + part.shape), beside


def swap_cores(block, flip_role=False):
    route = []
    for role in range(2):
        for dp in range(8):
            for core in range(2):
                low = dp % 2
                source = (role * 8 + dp) * 2 + core
                target_role = 1 - role if flip_role else role
                target = (target_role * 8 + dp - low + core) * 2 + low
                route.append((source, target))
    return lax.ppermute(block, ("role", "dp", "core"), route)


def gather_ring(block, before):
    me = lax.axis_index("dp")
    high = me - me % 2
    up, down = [block], [block]
    for step in range(3):
        up.append(rotate(up[-1], "dp", 1))
        down.append(rotate(down[-1], "dp", -1))
    before, up, down = lax.optimization_barrier((before, up, down))
    up.append(rotate(up[-1], "dp", 1))
    whole = jnp.zeros((8,) + block.shape, block.dtype)
    for step in range(5):
        whole = lax.dynamic_update_index_in_dim(whole, up[step], ((me + 8 - step) % 8) ^ high, 0)
    for step in range(1, 4):
        whole = lax.dynamic_update_index_in_dim(whole, down[step], ((me + step) % 8) ^ high, 0)
    return whole, before


def scatter_sum(parts):
    blocks = lax.all_to_all(parts, X + ("y",), 0, 0, tiled=True)
    return jnp.sum(blocks.astype(jnp.float32), axis=0)


def project_kernel(weight_ref, tokens_ref, out_ref):
    dims = (((1,), (1,)), ((), ()))
    total = lax.dot_general(
        weight_ref[0, 0, 0], tokens_ref[0, 0, 0], dims, preferred_element_type=jnp.float32
    )
    total += lax.dot_general(
        weight_ref[0, 1, 0], tokens_ref[0, 1, 0], dims, preferred_element_type=jnp.float32
    )
    out_ref[0, 0] = total.astype(out_ref.dtype)


def project(weight, attended):
    part, depth = weight.shape[3:]
    tokens = attended.shape[3]

    def spec(array):
        pairs, _, roles = array.shape[:3]
        return pl.BlockSpec(
            (1, 2, 1) + array.shape[3:],
            lambda r, k: (k if pairs > 1 else 0, 0, r if roles > 1 else 0, 0, 0),
        )

    out = pl.pallas_call(
        project_kernel,
        grid=(2, 4),
        in_specs=[spec(weight), spec(attended)],
        out_specs=pl.BlockSpec((1, 1, part, tokens), lambda r, k: (r, k, 0, 0)),
        out_shape=jax.ShapeDtypeStruct((2, 4, part, tokens), jnp.bfloat16),
        compiler_params=pltpu.CompilerParams(vmem_limit_bytes=32 * 1024 * 1024),
        cost_estimate=pl.CostEstimate(
            flops=32 * part * depth * tokens, bytes_accessed=6_000_000, transcendentals=0
        ),
    )(weight, attended)
    return out.reshape(8, part, tokens)


def normalize(state, norm_gain):
    values = state.astype(jnp.float32)
    mean_square = jnp.mean(values * values, axis=0, keepdims=True)
    return (values * lax.rsqrt(mean_square + NORM_EPS) * norm_gain[:, None]).astype(jnp.bfloat16)


def revise(current_state, update, pick_codes, mask_values):
    values = current_state.astype(jnp.float32)
    masked = jnp.broadcast_to(mask_values.astype(jnp.float32)[:, None], values.shape)
    return jnp.where(
        pick_codes == 1, values + update, jnp.where(pick_codes == 2, masked, values)
    ).astype(jnp.bfloat16)


def attend(queries, cache_keys, cache_values, block_keys, block_values, prefix_lengths):
    score_scale = HEAD ** (-0.5)
    prefix_len = cache_keys.shape[1]
    prefix_scores = (
        jnp.einsum("rbgh,rph->rgbp", queries, cache_keys, preferred_element_type=jnp.float32)
        * score_scale
    )
    valid_keys = jnp.arange(prefix_len, dtype=jnp.int32)[None, :] < prefix_lengths[:, None]
    prefix_scores = jnp.where(valid_keys[:, None, None, :], prefix_scores, -jnp.inf)
    block_scores = (
        jnp.einsum("rbgh,rch->rgbc", queries, block_keys, preferred_element_type=jnp.float32)
        * score_scale
    )
    score_top = jnp.maximum(jnp.max(prefix_scores, axis=-1), jnp.max(block_scores, axis=-1))[
        ..., None
    ]
    prefix_exp = jnp.exp(prefix_scores - score_top)
    block_exp = jnp.exp(block_scores - score_top)
    denom_sum = (jnp.sum(prefix_exp, axis=-1) + jnp.sum(block_exp, axis=-1))[..., None]
    prefix_probs = (prefix_exp / denom_sum).astype(jnp.bfloat16)
    block_probs = (block_exp / denom_sum).astype(jnp.bfloat16)
    attended = jnp.einsum(
        "rgbp,rph->rbgh", prefix_probs, cache_values, preferred_element_type=jnp.float32
    )
    attended = attended + jnp.einsum(
        "rgbc,rch->rbgh", block_probs, block_values, preferred_element_type=jnp.float32
    )
    return attended.astype(jnp.bfloat16).reshape(queries.shape[0] * queries.shape[1], -1)


def on_device(
    learner_inputs,
    learner_cotangent,
    master_weight,
    first_moment,
    second_moment,
    query_weight,
    keyval_weight,
    prefix_cache,
    block_states,
    norm_gain,
    mask_vector,
    prefix_lengths,
    position_picks,
):
    bf16, f32 = jnp.bfloat16, jnp.float32
    role, core, dp = lax.axis_index("role"), lax.axis_index("core"), lax.axis_index("dp")
    rows, block_len, part = block_states.shape
    tokens = rows * block_len
    depth = learner_inputs.shape[1]
    out_scale = (HEADS * HEAD) ** (-0.5)

    cache_other = rotate(prefix_cache, "core", 1)
    cache_keys = jnp.where(core == 0, prefix_cache, cache_other)
    cache_values = jnp.where(core == 0, cache_other, prefix_cache)

    def mask_of(block):
        return lax.dynamic_slice_in_dim(mask_vector, block * part, part, 0)

    def attended_of(whole):
        normed = normalize(whole.reshape(-1, tokens), norm_gain)
        own_half = lax.dot_general(
            normed, keyval_weight, (((0,), (0,)), ((), ())), preferred_element_type=f32
        ).astype(bf16)
        other_half = rotate(own_half, "core", 1)
        queries = lax.dot_general(
            normed, query_weight, (((0,), (0,)), ((), ())), preferred_element_type=f32
        ).astype(bf16)
        block_keys = jnp.where(core == 0, own_half, other_half).reshape(rows, block_len, HEAD)
        block_values = jnp.where(core == 0, other_half, own_half).reshape(rows, block_len, HEAD)
        return attend(
            queries.reshape(rows, block_len, -1, HEAD),
            cache_keys,
            cache_values,
            block_keys,
            block_values,
            prefix_lengths,
        )
    cotangent = lax.all_gather(learner_cotangent, ("x0", "y", "core", "x1"), axis=1, tiled=True)
    whole, _ = gather_features(block_states.reshape(tokens, part).T, 0, 0)
    attended = attended_of(whole)
    both = jnp.stack([swap_cores(attended), swap_cores(attended, True)])
    attended_all, cotangent = gather_ring(both, cotangent)

    terms = lax.dot_general(
        cotangent, learner_inputs, (((0,), (0,)), ((), ())), preferred_element_type=f32
    ).astype(bf16)
    terms = terms.reshape(8, 2, part, depth)
    halves = lax.psum_scatter(terms, "dp", scatter_dimension=0, tiled=False)
    gradient = pick(halves, role).astype(f32) + rotate(pick(halves, 1 - role), "role", 1).astype(f32)
    new_weight, new_first, new_second = adam_update(
        gradient, master_weight.T, first_moment.T, second_moment.T
    )
    weight_part = new_weight.astype(bf16)
    weight_pair = pair_order(weight_part, rotate(weight_part, "core", 1), core, 0)

    partial = project(
        weight_pair.reshape(1, 2, 1, part, depth), attended_all.reshape(4, 2, 2, tokens, depth)
    )
    weight_half, partial = lax.optimization_barrier((swap_cores(weight_part), partial))
    weight_all = lax.all_gather(weight_half, "dp", axis=0)
    update = scatter_sum(partial).astype(bf16)
    route = []
    for source in range(256):
        r, d2, d1, d0, x1, x0, y, c = [source >> k & 1 for k in range(7, -1, -1)]
        target = [r ^ x1, d2 ^ x0, d1 ^ y, c, x1, x0, y, d0]
        route.append((source, sum(bit << 7 - k for k, bit in enumerate(target))))
    update = lax.ppermute(update, EVERY, route).astype(f32) * out_scale
    picks = position_picks.reshape(STEPS, 1, tokens)
    shift_x, shift_y = role * 2 + dp // 4, dp // 2 % 2
    block = ((lax.axis_index(X) ^ shift_x) * 2 + (lax.axis_index("y") ^ shift_y)) * 2 + core
    state = revise(pick(whole, block), update, picks[0], mask_of(block))

    whole, weight_all = gather_features(state, shift_x, shift_y, weight_all)
    attended = attended_of(whole)
    attended_pair = pair_order(attended, rotate(attended, "core", 1), core, 0)
    route = [(r * 2 + c, (1 - r) * 2 + 1 - c) for r in range(2) for c in range(2)]
    far = lax.ppermute(attended, ("role", "core"), route)
    far_pair = pair_order(rotate(attended, "role", 1), far, core, 0)
    attended_four = pair_order(attended_pair, far_pair, role, 1)
    partial = project(weight_all.reshape(4, 2, 1, part, depth), attended_four[None])
    update = scatter_sum(partial).astype(bf16)
    update = lax.ppermute(update, ("role", "x1"), [(0, 0), (1, 2), (2, 1), (3, 3)])
    block = lax.axis_index(TENSOR)
    state = revise(pick(whole, block), update.astype(f32) * out_scale, picks[1], mask_of(block))
    return (state.T.reshape(rows, block_len, part), new_weight.T, new_first.T, new_second.T)


def solution(mesh):
    fine = Mesh(mesh.devices.reshape(2, 8, 2, 2, 2, 2), EVERY)
    weights = P(TENSOR, RD)
    return jax.shard_map(
        on_device,
        mesh=fine,
        in_specs=(
            P(RD, TENSOR),
            P(RD, TENSOR),
            weights,
            weights,
            weights,
            P(None, TENSOR),
            P(None, TENSOR),
            P(RD, None, TENSOR),
            P(RD, None, TENSOR),
            P(),
            P(),
            P(RD),
            P(None, RD, None),
        ),
        out_specs=(P(RD, None, TENSOR), weights, weights, weights),
        check_vma=False,
    )
```

```python
import jax
import jax.numpy as jnp
from jax import lax
from jax.experimental import pallas as pl
from jax.experimental.pallas import tpu as pltpu
from jax.sharding import Mesh, PartitionSpec as P

HEADS = 64
HEAD = 128
STEPS = 2

BETA_ONE = 0.9
BETA_TWO = 0.95
ADAM_EPS = 1e-08
LEARN_RATE = 0.5
DECAY_RATE = 0.1
STEP_COUNT = 50
NORM_EPS = 1e-06

RD = ("role", "dp")
X = ("x1", "x0")
TENSOR = X + ("y", "core")
EVERY = RD + TENSOR


def rotate(block, axis, shift):
    count = 4 if axis == X else lax.axis_size(axis)
    return lax.ppermute(block, axis, [(low, (low + shift) % count) for low in range(count)])


def pick(blocks, index):
    return lax.dynamic_index_in_dim(blocks, index, 0, keepdims=False)


def pair_order(own, other, index, axis):
    return jnp.where(index == 0, jnp.stack([own, other], axis), jnp.stack([other, own], axis))


def adam_update(gradient, master_weight, first_moment, second_moment):
    first_new = BETA_ONE * first_moment + (1.0 - BETA_ONE) * gradient
    second_new = BETA_TWO * second_moment + (1.0 - BETA_TWO) * gradient * gradient
    first_hat = first_new / (1.0 - BETA_ONE**STEP_COUNT)
    second_hat = second_new / (1.0 - BETA_TWO**STEP_COUNT)
    weight_new = master_weight - LEARN_RATE * (
        first_hat / (jnp.sqrt(second_hat) + ADAM_EPS) + DECAY_RATE * master_weight
    )
    return (weight_new, first_new, second_new)


def gather_rows(rows, shift_x, beside=None):
    ix, ic = lax.axis_index(X), lax.axis_index("core")
    ahead, back, across = rotate(rows, X, 1), rotate(rows, X, -1), rotate(rows, X, 2)
    square = jnp.zeros((4,) + rows.shape, rows.dtype)
    square = lax.dynamic_update_index_in_dim(square, rows, ix ^ shift_x, 0)
    square = lax.dynamic_update_index_in_dim(square, ahead, ((ix + 3) % 4) ^ shift_x, 0)
    square = lax.dynamic_update_index_in_dim(square, back, ((ix + 1) % 4) ^ shift_x, 0)
    square = lax.dynamic_update_index_in_dim(square, across, ((ix + 2) % 4) ^ shift_x, 0)
    square, beside = lax.optimization_barrier((square, beside))
    return pair_order(square, rotate(square, "core", 1), ic, 2), beside


def swap_cores(block, flip_role=False):
    route = []
    for role in range(2):
        for dp in range(8):
            for core in range(2):
                low = dp % 2
                source = (role * 8 + dp) * 2 + core
                target_role = 1 - role if flip_role else role
                target = (target_role * 8 + dp - low + core) * 2 + low
                route.append((source, target))
    return lax.ppermute(block, ("role", "dp", "core"), route)


def gather_ring(block, before):
    me = lax.axis_index("dp")
    high = me - me % 2
    up, down = [block], [block]
    for step in range(3):
        up.append(rotate(up[-1], "dp", 1))
        down.append(rotate(down[-1], "dp", -1))
    before, up, down = lax.optimization_barrier((before, up, down))
    up.append(rotate(up[-1], "dp", 1))
    whole = jnp.zeros((8,) + block.shape, block.dtype)
    for step in range(5):
        whole = lax.dynamic_update_index_in_dim(whole, up[step], ((me + 8 - step) % 8) ^ high, 0)
    for step in range(1, 4):
        whole = lax.dynamic_update_index_in_dim(whole, down[step], ((me + step) % 8) ^ high, 0)
    return whole, before


def scatter_sum(parts):
    blocks = lax.all_to_all(parts, X + ("y",), 0, 0, tiled=True)
    return jnp.sum(blocks.astype(jnp.float32), axis=0)


def gradient_kernel(
    cotangent_ref, inputs_ref, out_ref, cotangents, inputs, outs, inputs_sem, cotangent_sems, out_sems
):
    steps, block = cotangents.shape[:2]

    def inputs_copy():
        return pltpu.make_async_copy(inputs_ref, inputs, inputs_sem)

    def cotangent_copy(i):
        return pltpu.make_async_copy(
            cotangent_ref.at[pl.ds(i * block, block)], cotangents.at[i], cotangent_sems.at[i]
        )

    def out_copy(i):
        place = out_ref.at[pl.ds(2 * (i % (steps // 2)), 2), i // (steps // 2)]
        return pltpu.make_async_copy(outs.at[i], place, out_sems.at[i])

    cotangent_copy(0).start()
    inputs_copy().start()
    for i in range(1, steps):
        cotangent_copy(i).start()
    inputs_copy().wait()

    def step(i, carry):
        cotangent_copy(i).wait()
        terms = jnp.dot(cotangents[i], inputs[...], preferred_element_type=jnp.float32)
        outs[i] = terms.astype(outs.dtype).reshape(outs.shape[1:])
        out_copy(i).start()
        return carry

    lax.fori_loop(0, steps, step, 0)
    for i in range(steps):
        out_copy(i).wait()


def gradient_terms(cotangent, inputs):
    tokens, depth = inputs.shape
    part = cotangent.shape[0] // 16
    steps = 8
    return pl.pallas_call(
        gradient_kernel,
        in_specs=[pl.BlockSpec(memory_space=pl.ANY)] * 2,
        out_specs=pl.BlockSpec(memory_space=pl.ANY),
        out_shape=jax.ShapeDtypeStruct((8, 2, part, depth), jnp.bfloat16),
        scratch_shapes=[
            pltpu.VMEM((steps, 2 * part, tokens), jnp.bfloat16),
            pltpu.VMEM((tokens, depth), jnp.bfloat16),
            pltpu.VMEM((steps, 2, part, depth), jnp.bfloat16),
            pltpu.SemaphoreType.DMA,
            pltpu.SemaphoreType.DMA((steps,)),
            pltpu.SemaphoreType.DMA((steps,)),
        ],
        compiler_params=pltpu.CompilerParams(vmem_limit_bytes=60 * 1024 * 1024),
        cost_estimate=pl.CostEstimate(
            flops=2 * 16 * part * tokens * depth, bytes_accessed=17_000_000, transcendentals=0
        ),
    )(cotangent, inputs)


def project_block(weight, attended, out_ref, n):
    dims = (((1,), (1,)), ((), ()))
    total = lax.dot_general(weight[0], attended[0], dims, preferred_element_type=jnp.float32)
    total += lax.dot_general(weight[1], attended[1], dims, preferred_element_type=jnp.float32)
    out_ref[n] = total.astype(out_ref.dtype)


def project_all_kernel(weight_ref, tokens_ref, out_ref):
    for n in range(8):
        project_block(weight_ref, tokens_ref.at[n % 4, :, n // 4], out_ref, n)


def project_all(weight, attended):
    part, depth = weight.shape[1:]
    tokens = attended.shape[3]
    return pl.pallas_call(
        project_all_kernel,
        out_shape=jax.ShapeDtypeStruct((8, part, tokens), jnp.bfloat16),
        compiler_params=pltpu.CompilerParams(vmem_limit_bytes=32 * 1024 * 1024),
        cost_estimate=pl.CostEstimate(
            flops=32 * part * depth * tokens, bytes_accessed=3_000_000, transcendentals=0
        ),
    )(weight, attended)


def project_own_kernel(weight_ref, tokens_ref, out_ref, weights, sems):
    copies = [
        pltpu.make_async_copy(weight_ref.at[k], weights.at[k], sems.at[k]) for k in range(4)
    ]
    for copy in copies:
        copy.start()
    for k in range(4):
        copies[k].wait()
        for r in range(2):
            project_block(weights.at[k], tokens_ref.at[:, r], out_ref, r * 4 + k)


def project_own(weight, attended):
    part, depth = weight.shape[2:]
    tokens = attended.shape[2]
    vmem = pl.BlockSpec(memory_space=pltpu.VMEM)
    return pl.pallas_call(
        project_own_kernel,
        in_specs=[pl.BlockSpec(memory_space=pl.ANY), vmem],
        out_specs=vmem,
        out_shape=jax.ShapeDtypeStruct((8, part, tokens), jnp.bfloat16),
        scratch_shapes=[
            pltpu.VMEM(weight.shape, weight.dtype),
            pltpu.SemaphoreType.DMA((4,)),
        ],
        compiler_params=pltpu.CompilerParams(vmem_limit_bytes=60 * 1024 * 1024),
        cost_estimate=pl.CostEstimate(
            flops=32 * part * depth * tokens, bytes_accessed=4_000_000, transcendentals=0
        ),
    )(weight, attended)


def normalize(state, norm_gain):
    values = state.astype(jnp.float32)
    mean_square = jnp.mean(values * values, axis=0, keepdims=True)
    return (values * lax.rsqrt(mean_square + NORM_EPS) * norm_gain[:, None]).astype(jnp.bfloat16)


def revise(current_state, update, pick_codes, mask_values):
    values = current_state.astype(jnp.float32)
    masked = jnp.broadcast_to(mask_values.astype(jnp.float32)[..., None], values.shape)
    return jnp.where(
        pick_codes == 1, values + update, jnp.where(pick_codes == 2, masked, values)
    ).astype(jnp.bfloat16)


def attend(queries, cache_keys, cache_values, block_keys, block_values, prefix_lengths):
    score_scale = HEAD ** (-0.5)
    prefix_len = cache_keys.shape[1]
    prefix_scores = (
        jnp.einsum("rbgh,rph->rgbp", queries, cache_keys, preferred_element_type=jnp.float32)
        * score_scale
    )
    valid_keys = jnp.arange(prefix_len, dtype=jnp.int32)[None, :] < prefix_lengths[:, None]
    prefix_scores = jnp.where(valid_keys[:, None, None, :], prefix_scores, -jnp.inf)
    block_scores = (
        jnp.einsum("rbgh,rch->rgbc", queries, block_keys, preferred_element_type=jnp.float32)
        * score_scale
    )
    score_top = jnp.maximum(jnp.max(prefix_scores, axis=-1), jnp.max(block_scores, axis=-1))[
        ..., None
    ]
    prefix_exp = jnp.exp(prefix_scores - score_top)
    block_exp = jnp.exp(block_scores - score_top)
    denom_sum = (jnp.sum(prefix_exp, axis=-1) + jnp.sum(block_exp, axis=-1))[..., None]
    prefix_probs = (prefix_exp / denom_sum).astype(jnp.bfloat16)
    block_probs = (block_exp / denom_sum).astype(jnp.bfloat16)
    attended = jnp.einsum(
        "rgbp,rph->rbgh", prefix_probs, cache_values, preferred_element_type=jnp.float32
    )
    attended = attended + jnp.einsum(
        "rgbc,rch->rbgh", block_probs, block_values, preferred_element_type=jnp.float32
    )
    return attended.astype(jnp.bfloat16).reshape(queries.shape[0] * queries.shape[1], -1)


def on_device(
    learner_inputs,
    learner_cotangent,
    master_weight,
    first_moment,
    second_moment,
    query_weight,
    keyval_weight,
    prefix_cache,
    block_states,
    norm_gain,
    mask_vector,
    prefix_lengths,
    position_picks,
):
    bf16, f32 = jnp.bfloat16, jnp.float32
    role, core, dp = lax.axis_index("role"), lax.axis_index("core"), lax.axis_index("dp")
    row_count, block_len, part = block_states.shape
    tokens = row_count * block_len
    depth = learner_inputs.shape[1]
    out_scale = (HEADS * HEAD) ** (-0.5)

    cache_other = rotate(prefix_cache, "core", 1)
    cache_keys = jnp.where(core == 0, prefix_cache, cache_other)
    cache_values = jnp.where(core == 0, cache_other, prefix_cache)

    masks = mask_vector.reshape(4, 2, 2, part)
    ix, iy = lax.axis_index(X), lax.axis_index("y")

    def rows_of(blocks, index):
        return lax.dynamic_index_in_dim(pick(blocks, index), core, 1, keepdims=False)

    def attended_of(whole):
        normed = normalize(whole.reshape(-1, tokens), norm_gain)
        own_half = lax.dot_general(
            normed, keyval_weight, (((0,), (0,)), ((), ())), preferred_element_type=f32
        ).astype(bf16)
        other_half = rotate(own_half, "core", 1)
        queries = lax.dot_general(
            normed, query_weight, (((0,), (0,)), ((), ())), preferred_element_type=f32
        ).astype(bf16)
        block_keys = jnp.where(core == 0, own_half, other_half).reshape(row_count, block_len, HEAD)
        block_values = jnp.where(core == 0, other_half, own_half).reshape(row_count, block_len, HEAD)
        return attend(
            queries.reshape(row_count, block_len, -1, HEAD),
            cache_keys,
            cache_values,
            block_keys,
            block_values,
            prefix_lengths,
        )

    cotangent = lax.all_gather(learner_cotangent, TENSOR, axis=1, tiled=True)
    state = block_states.reshape(tokens, part).T
    whole, _ = gather_rows(pair_order(state, rotate(state, "y", 1), iy, 0), 0)
    attended = attended_of(whole)
    both = jnp.stack([swap_cores(attended), swap_cores(attended, True)])
    attended_all, cotangent = gather_ring(both, cotangent)

    terms = gradient_terms(cotangent.T, learner_inputs)
    halves = lax.psum_scatter(terms, "dp", scatter_dimension=0, tiled=False)
    gradient = pick(halves, role).astype(f32) + rotate(pick(halves, 1 - role), "role", 1).astype(f32)
    new_weight, new_first, new_second = adam_update(
        gradient, master_weight.T, first_moment.T, second_moment.T
    )
    weight_part = new_weight.astype(bf16)
    weight_pair = pair_order(weight_part, rotate(weight_part, "core", 1), core, 0)

    partial = project_all(weight_pair, attended_all.reshape(4, 2, 2, tokens, depth))
    weight_half, partial = lax.optimization_barrier((swap_cores(weight_part), partial))
    weight_all = lax.all_gather(weight_half, "dp", axis=0)
    update = scatter_sum(partial).astype(bf16)

    def deal(flip):
        route = []
        for source in range(256):
            r, d2, d1, d0, x1, x0, y, c = [source >> k & 1 for k in range(7, -1, -1)]
            target = [r ^ x1, d2 ^ x0, d1 ^ y, c, x1, x0, y ^ flip, d0]
            route.append((source, sum(bit << 7 - k for k, bit in enumerate(target))))
        return lax.ppermute(update, EVERY, route)

    shift_x, shift_y = role * 2 + dp // 4, dp // 2 % 2
    update = pair_order(deal(0), deal(1), iy ^ shift_y, 0).astype(f32) * out_scale
    picks = position_picks.reshape(STEPS, 1, tokens)
    rows = revise(rows_of(whole, ix ^ shift_x), update, picks[0], rows_of(masks, ix ^ shift_x))

    whole, weight_all = gather_rows(rows, shift_x, weight_all)
    attended = attended_of(whole)
    attended_pair = pair_order(attended, rotate(attended, "core", 1), core, 0)
    route = [(r * 2 + c, (1 - r) * 2 + 1 - c) for r in range(2) for c in range(2)]
    far = lax.ppermute(attended, ("role", "core"), route)
    far_pair = pair_order(rotate(attended, "role", 1), far, core, 0)
    attended_four = pair_order(attended_pair, far_pair, role, 1)
    partial = project_own(weight_all.reshape(4, 2, part, depth), attended_four)
    update = scatter_sum(partial).astype(bf16)
    update = lax.ppermute(update, ("role", "x1"), [(0, 0), (1, 2), (2, 1), (3, 3)])
    state = pick(rows_of(whole, ix), iy)
    state = revise(state, update.astype(f32) * out_scale, picks[1], pick(rows_of(masks, ix), iy))
    return (state.T.reshape(row_count, block_len, part), new_weight.T, new_first.T, new_second.T)


def solution(mesh):
    fine = Mesh(mesh.devices.reshape(2, 8, 2, 2, 2, 2), EVERY)
    weights = P(TENSOR, RD)
    return jax.shard_map(
        on_device,
        mesh=fine,
        in_specs=(
            P(RD, TENSOR),
            P(RD, TENSOR),
            weights,
            weights,
            weights,
            P(None, TENSOR),
            P(None, TENSOR),
            P(RD, None, TENSOR),
            P(RD, None, TENSOR),
            P(),
            P(),
            P(RD),
            P(None, RD, None),
        ),
        out_specs=(P(RD, None, TENSOR), weights, weights, weights),
        check_vma=False,
    )
```

```python
import jax
import jax.numpy as jnp
from jax import lax
from jax.experimental import pallas as pl
from jax.experimental.pallas import tpu as pltpu
from jax.sharding import Mesh, PartitionSpec as P

HEADS = 64
HEAD = 128
STEPS = 2

BETA_ONE = 0.9
BETA_TWO = 0.95
ADAM_EPS = 1e-08
LEARN_RATE = 0.5
DECAY_RATE = 0.1
STEP_COUNT = 50
NORM_EPS = 1e-06

RD = ("role", "dp")
X = ("x1", "x0")
TENSOR = X + ("y", "core")
EVERY = RD + TENSOR


def rotate(block, axis, shift):
    count = 4 if axis == X else lax.axis_size(axis)
    return lax.ppermute(block, axis, [(low, (low + shift) % count) for low in range(count)])


def pick(blocks, index):
    return lax.dynamic_index_in_dim(blocks, index, 0, keepdims=False)


def pair_order(own, other, index, axis):
    return jnp.where(index == 0, jnp.stack([own, other], axis), jnp.stack([other, own], axis))


def adam_update(gradient, master_weight, first_moment, second_moment):
    first_new = BETA_ONE * first_moment + (1.0 - BETA_ONE) * gradient
    second_new = BETA_TWO * second_moment + (1.0 - BETA_TWO) * gradient * gradient
    first_hat = first_new / (1.0 - BETA_ONE**STEP_COUNT)
    second_hat = second_new / (1.0 - BETA_TWO**STEP_COUNT)
    weight_new = master_weight - LEARN_RATE * (
        first_hat / (jnp.sqrt(second_hat) + ADAM_EPS) + DECAY_RATE * master_weight
    )
    return (weight_new, first_new, second_new)


def gather_rows(rows, shift_x, beside=None):
    ix = lax.axis_index(X)
    ahead, back, across = rotate(rows, X, 1), rotate(rows, X, -1), rotate(rows, X, 2)
    square = jnp.zeros((4,) + rows.shape, rows.dtype)
    square = lax.dynamic_update_index_in_dim(square, rows, ix ^ shift_x, 0)
    square = lax.dynamic_update_index_in_dim(square, ahead, ((ix + 3) % 4) ^ shift_x, 0)
    square = lax.dynamic_update_index_in_dim(square, back, ((ix + 1) % 4) ^ shift_x, 0)
    square = lax.dynamic_update_index_in_dim(square, across, ((ix + 2) % 4) ^ shift_x, 0)
    return lax.optimization_barrier((square, beside))


def swap_cores(block, flip_role=False):
    route = []
    for role in range(2):
        for dp in range(8):
            for core in range(2):
                low = dp % 2
                source = (role * 8 + dp) * 2 + core
                target_role = 1 - role if flip_role else role
                target = (target_role * 8 + dp - low + core) * 2 + low
                route.append((source, target))
    return lax.ppermute(block, ("role", "dp", "core"), route)


def gather_ring(block, before):
    me = lax.axis_index("dp")
    high = me - me % 2
    up, down = [block], [block]
    for step in range(3):
        up.append(rotate(up[-1], "dp", 1))
        down.append(rotate(down[-1], "dp", -1))
    before, up, down = lax.optimization_barrier((before, up, down))
    up.append(rotate(up[-1], "dp", 1))
    whole = jnp.zeros((8,) + block.shape, block.dtype)
    for step in range(5):
        whole = lax.dynamic_update_index_in_dim(whole, up[step], ((me + 8 - step) % 8) ^ high, 0)
    for step in range(1, 4):
        whole = lax.dynamic_update_index_in_dim(whole, down[step], ((me + step) % 8) ^ high, 0)
    return whole, before


def scatter_sum(parts):
    blocks = lax.all_to_all(parts, X + ("y",), 0, 0, tiled=True)
    return jnp.sum(blocks.astype(jnp.float32), axis=0)


def gradient_kernel(cotangent_ref, inputs_ref, out_ref):
    terms = jnp.dot(cotangent_ref[...], inputs_ref[...], preferred_element_type=jnp.float32)
    out_ref[...] = terms.astype(out_ref.dtype).reshape(out_ref.shape)


def gradient_terms(cotangent, inputs):
    tokens, depth = inputs.shape
    part = cotangent.shape[0] // 16
    return pl.pallas_call(
        gradient_kernel,
        grid=(4,),
        in_specs=[
            pl.BlockSpec((4 * part, tokens), lambda i: (i, 0)),
            pl.BlockSpec((tokens, depth), lambda i: (0, 0)),
        ],
        out_specs=pl.BlockSpec((4, 1, part, depth), lambda i: (i % 2, i // 2, 0, 0)),
        out_shape=jax.ShapeDtypeStruct((8, 2, part, depth), jnp.bfloat16),
        compiler_params=pltpu.CompilerParams(vmem_limit_bytes=60 * 1024 * 1024),
        cost_estimate=pl.CostEstimate(
            flops=2 * 16 * part * tokens * depth, bytes_accessed=17_000_000, transcendentals=0
        ),
    )(cotangent, inputs)


def project_block(weight, attended, out_ref, n):
    dims = (((1,), (1,)), ((), ()))
    total = lax.dot_general(weight[0], attended[0], dims, preferred_element_type=jnp.float32)
    total += lax.dot_general(weight[1], attended[1], dims, preferred_element_type=jnp.float32)
    out_ref[n] = total.astype(out_ref.dtype)


def project_all_kernel(weight_ref, tokens_ref, out_ref):
    for n in range(8):
        project_block(weight_ref, tokens_ref.at[n % 4, :, n // 4], out_ref, n)


def project_all(weight, attended):
    part, depth = weight.shape[1:]
    tokens = attended.shape[3]
    return pl.pallas_call(
        project_all_kernel,
        out_shape=jax.ShapeDtypeStruct((8, part, tokens), jnp.bfloat16),
        compiler_params=pltpu.CompilerParams(vmem_limit_bytes=32 * 1024 * 1024),
        cost_estimate=pl.CostEstimate(
            flops=32 * part * depth * tokens, bytes_accessed=3_000_000, transcendentals=0
        ),
    )(weight, attended)


def project_own_kernel(weight_ref, tokens_ref, out_ref):
    project_block(weight_ref.at[0], tokens_ref.at[:, 0], out_ref.at[0], 0)


def project_own(weight, attended):
    part, depth = weight.shape[2:]
    tokens = attended.shape[2]
    out = pl.pallas_call(
        project_own_kernel,
        grid=(2, 4),
        in_specs=[
            pl.BlockSpec((1, 2, part, depth), lambda r, k: (k, 0, 0, 0)),
            pl.BlockSpec((2, 1, tokens, depth), lambda r, k: (0, r, 0, 0)),
        ],
        out_specs=pl.BlockSpec((1, 1, part, tokens), lambda r, k: (r, k, 0, 0)),
        out_shape=jax.ShapeDtypeStruct((2, 4, part, tokens), jnp.bfloat16),
        compiler_params=pltpu.CompilerParams(vmem_limit_bytes=32 * 1024 * 1024),
        cost_estimate=pl.CostEstimate(
            flops=32 * part * depth * tokens, bytes_accessed=4_000_000, transcendentals=0
        ),
    )(weight, attended)
    return out.reshape(8, part, tokens)


def half_products(square, gain, query_weight, keyval_weight):
    values = square.astype(jnp.float32)
    squares = jnp.sum(values * values, axis=(0, 1, 2))
    scaled = (values * gain[..., None]).astype(jnp.bfloat16).reshape(-1, square.shape[-1])
    dims = (((0,), (0,)), ((), ()))
    queries = lax.dot_general(scaled, query_weight, dims, preferred_element_type=jnp.float32)
    keyvals = lax.dot_general(scaled, keyval_weight, dims, preferred_element_type=jnp.float32)
    return squares, queries, keyvals


def revise(current_state, update, pick_codes, mask_values):
    values = current_state.astype(jnp.float32)
    masked = jnp.broadcast_to(mask_values.astype(jnp.float32)[..., None], values.shape)
    return jnp.where(
        pick_codes == 1, values + update, jnp.where(pick_codes == 2, masked, values)
    ).astype(jnp.bfloat16)


def attend(queries, cache_keys, cache_values, block_keys, block_values, prefix_lengths):
    score_scale = HEAD ** (-0.5)
    prefix_len = cache_keys.shape[1]
    prefix_scores = (
        jnp.einsum("rbgh,rph->rgbp", queries, cache_keys, preferred_element_type=jnp.float32)
        * score_scale
    )
    valid_keys = jnp.arange(prefix_len, dtype=jnp.int32)[None, :] < prefix_lengths[:, None]
    prefix_scores = jnp.where(valid_keys[:, None, None, :], prefix_scores, -jnp.inf)
    block_scores = (
        jnp.einsum("rbgh,rch->rgbc", queries, block_keys, preferred_element_type=jnp.float32)
        * score_scale
    )
    score_top = jnp.maximum(jnp.max(prefix_scores, axis=-1), jnp.max(block_scores, axis=-1))[
        ..., None
    ]
    prefix_exp = jnp.exp(prefix_scores - score_top)
    block_exp = jnp.exp(block_scores - score_top)
    denom_sum = (jnp.sum(prefix_exp, axis=-1) + jnp.sum(block_exp, axis=-1))[..., None]
    prefix_probs = (prefix_exp / denom_sum).astype(jnp.bfloat16)
    block_probs = (block_exp / denom_sum).astype(jnp.bfloat16)
    attended = jnp.einsum(
        "rgbp,rph->rbgh", prefix_probs, cache_values, preferred_element_type=jnp.float32
    )
    attended = attended + jnp.einsum(
        "rgbc,rch->rbgh", block_probs, block_values, preferred_element_type=jnp.float32
    )
    return attended.astype(jnp.bfloat16).reshape(queries.shape[0] * queries.shape[1], -1)


def on_device(
    learner_inputs,
    learner_cotangent,
    master_weight,
    first_moment,
    second_moment,
    query_weight,
    keyval_weight,
    prefix_cache,
    block_states,
    norm_gain,
    mask_vector,
    prefix_lengths,
    position_picks,
):
    bf16, f32 = jnp.bfloat16, jnp.float32
    role, core, dp = lax.axis_index("role"), lax.axis_index("core"), lax.axis_index("dp")
    row_count, block_len, part = block_states.shape
    tokens = row_count * block_len
    depth = learner_inputs.shape[1]
    out_scale = (HEADS * HEAD) ** (-0.5)

    cache_other = rotate(prefix_cache, "core", 1)
    cache_keys = jnp.where(core == 0, prefix_cache, cache_other)
    cache_values = jnp.where(core == 0, cache_other, prefix_cache)

    ix, iy = lax.axis_index(X), lax.axis_index("y")

    def half_of(array, which):
        blocks = array.reshape((4, 2, 2, part) + array.shape[1:])
        return lax.dynamic_index_in_dim(blocks, which, 2, keepdims=False)

    masks = half_of(mask_vector, core)
    sides = []
    for which in (core, 1 - core):
        sides.append(
            (
                half_of(norm_gain, which),
                half_of(query_weight, which).reshape(-1, query_weight.shape[1]),
                half_of(keyval_weight, which).reshape(-1, keyval_weight.shape[1]),
            )
        )
    sides = lax.optimization_barrier(sides)

    def attended_of(square):
        other = rotate(square, "core", 1)
        halves = [half_products(half, *side) for half, side in zip((square, other), sides)]
        squares, queries, keyvals = [sum(pair) for pair in zip(*halves)]
        factor = lax.rsqrt(squares / (16 * part) + NORM_EPS)[:, None]
        queries = (queries * factor).astype(bf16)
        own_half = (keyvals * factor).astype(bf16)
        other_half = rotate(own_half, "core", 1)
        block_keys = jnp.where(core == 0, own_half, other_half).reshape(row_count, block_len, HEAD)
        block_values = jnp.where(core == 0, other_half, own_half).reshape(row_count, block_len, HEAD)
        return attend(
            queries.reshape(row_count, block_len, -1, HEAD),
            cache_keys,
            cache_values,
            block_keys,
            block_values,
            prefix_lengths,
        )

    cotangent = lax.all_gather(learner_cotangent, TENSOR, axis=1, tiled=True)
    state = block_states.reshape(tokens, part).T
    square, _ = gather_rows(pair_order(state, rotate(state, "y", 1), iy, 0), 0)
    attended = attended_of(square)
    both = jnp.stack([swap_cores(attended), swap_cores(attended, True)])
    attended_all, cotangent = gather_ring(both, cotangent)

    terms = gradient_terms(cotangent.T, learner_inputs)
    halves = lax.psum_scatter(terms, "dp", scatter_dimension=0, tiled=False)
    halves, attended_all = lax.optimization_barrier((halves, attended_all))
    gradient = pick(halves, role).astype(f32) + rotate(pick(halves, 1 - role), "role", 1).astype(f32)
    new_weight, new_first, new_second = adam_update(
        gradient, master_weight.T, first_moment.T, second_moment.T
    )
    weight_part = new_weight.astype(bf16)
    weight_pair = pair_order(weight_part, rotate(weight_part, "core", 1), core, 0)

    partial = project_all(weight_pair, attended_all.reshape(4, 2, 2, tokens, depth))
    weight_half, partial = lax.optimization_barrier((swap_cores(weight_part), partial))
    weight_all = lax.all_gather(weight_half, "dp", axis=0)
    update = scatter_sum(partial).astype(bf16)

    def deal(flip):
        route = []
        for source in range(256):
            r, d2, d1, d0, x1, x0, y, c = [source >> k & 1 for k in range(7, -1, -1)]
            target = [r ^ x1, d2 ^ x0, d1 ^ y, c, x1, x0, y ^ flip, d0]
            route.append((source, sum(bit << 7 - k for k, bit in enumerate(target))))
        return lax.ppermute(update, EVERY, route)

    shift_x, shift_y = role * 2 + dp // 4, dp // 2 % 2
    update = pair_order(deal(0), deal(1), iy ^ shift_y, 0).astype(f32) * out_scale
    picks = position_picks.reshape(STEPS, 1, tokens)
    rows = revise(pick(square, ix ^ shift_x), update, picks[0], pick(masks, ix ^ shift_x))

    square, weight_all = gather_rows(rows, shift_x, weight_all)
    attended = attended_of(square)
    attended_pair = pair_order(attended, rotate(attended, "core", 1), core, 0)
    route = [(r * 2 + c, (1 - r) * 2 + 1 - c) for r in range(2) for c in range(2)]
    far = lax.ppermute(attended, ("role", "core"), route)
    far_pair = pair_order(rotate(attended, "role", 1), far, core, 0)
    attended_four = pair_order(attended_pair, far_pair, role, 1)
    partial = project_own(weight_all.reshape(4, 2, part, depth), attended_four)
    update = scatter_sum(partial).astype(bf16)
    update = lax.ppermute(update, ("role", "x1"), [(0, 0), (1, 2), (2, 1), (3, 3)])
    state = pick(pick(square, ix), iy)
    state = revise(state, update.astype(f32) * out_scale, picks[1], pick(pick(masks, ix), iy))
    return (state.T.reshape(row_count, block_len, part), new_weight.T, new_first.T, new_second.T)


def solution(mesh):
    fine = Mesh(mesh.devices.reshape(2, 8, 2, 2, 2, 2), EVERY)
    weights = P(TENSOR, RD)
    return jax.shard_map(
        on_device,
        mesh=fine,
        in_specs=(
            P(RD, TENSOR),
            P(RD, TENSOR),
            weights,
            weights,
            weights,
            P(None, TENSOR),
            P(None, TENSOR),
            P(RD, None, TENSOR),
            P(RD, None, TENSOR),
            P(),
            P(),
            P(RD),
            P(None, RD, None),
        ),
        out_specs=(P(RD, None, TENSOR), weights, weights, weights),
        check_vma=False,
    )
```

```python
import jax
import jax.numpy as jnp
from jax import lax
from jax.experimental import pallas as pl
from jax.experimental.pallas import tpu as pltpu
from jax.sharding import Mesh, PartitionSpec as P

HEADS = 64
HEAD = 128
STEPS = 2

BETA_ONE = 0.9
BETA_TWO = 0.95
ADAM_EPS = 1e-08
LEARN_RATE = 0.5
DECAY_RATE = 0.1
STEP_COUNT = 50
NORM_EPS = 1e-06

RD = ("role", "dp")
X = ("x1", "x0")
TENSOR = X + ("y", "core")
EVERY = RD + TENSOR


def rotate(block, axis, shift):
    count = 4 if axis == X else lax.axis_size(axis)
    return lax.ppermute(block, axis, [(low, (low + shift) % count) for low in range(count)])


def pick(blocks, index):
    return lax.dynamic_index_in_dim(blocks, index, 0, keepdims=False)


def pair_order(own, other, index, axis):
    return jnp.where(index == 0, jnp.stack([own, other], axis), jnp.stack([other, own], axis))


def adam_update(gradient, master_weight, first_moment, second_moment):
    first_new = BETA_ONE * first_moment + (1.0 - BETA_ONE) * gradient
    second_new = BETA_TWO * second_moment + (1.0 - BETA_TWO) * gradient * gradient
    first_hat = first_new / (1.0 - BETA_ONE**STEP_COUNT)
    second_hat = second_new / (1.0 - BETA_TWO**STEP_COUNT)
    weight_new = master_weight - LEARN_RATE * (
        first_hat / (jnp.sqrt(second_hat) + ADAM_EPS) + DECAY_RATE * master_weight
    )
    return (weight_new, first_new, second_new)


def gather_rows(rows):
    ix, ic = lax.axis_index(X), lax.axis_index("core")
    ahead, back, across = rotate(rows, X, 1), rotate(rows, X, -1), rotate(rows, X, 2)
    square = jnp.zeros((4,) + rows.shape, rows.dtype)
    square = lax.dynamic_update_index_in_dim(square, rows, ix, 0)
    square = lax.dynamic_update_index_in_dim(square, ahead, (ix + 3) % 4, 0)
    square = lax.dynamic_update_index_in_dim(square, back, (ix + 1) % 4, 0)
    square = lax.dynamic_update_index_in_dim(square, across, (ix + 2) % 4, 0)
    return square, pair_order(square, rotate(square, "core", 1), ic, 2)


def swap_cores(block, flip_role=False):
    route = []
    for role in range(2):
        for dp in range(8):
            for core in range(2):
                low = dp % 2
                source = (role * 8 + dp) * 2 + core
                target_role = 1 - role if flip_role else role
                target = (target_role * 8 + dp - low + core) * 2 + low
                route.append((source, target))
    return lax.ppermute(block, ("role", "dp", "core"), route)


def gather_ring(block, before):
    me = lax.axis_index("dp")
    high = me - me % 2
    up, down = [block], [block]
    for step in range(3):
        up.append(rotate(up[-1], "dp", 1))
        down.append(rotate(down[-1], "dp", -1))
    before, up, down = lax.optimization_barrier((before, up, down))
    up.append(rotate(up[-1], "dp", 1))
    whole = jnp.zeros((8,) + block.shape, block.dtype)
    for step in range(5):
        whole = lax.dynamic_update_index_in_dim(whole, up[step], ((me + 8 - step) % 8) ^ high, 0)
    for step in range(1, 4):
        whole = lax.dynamic_update_index_in_dim(whole, down[step], ((me + step) % 8) ^ high, 0)
    return whole, before


def scatter_sum(parts):
    blocks = lax.all_to_all(parts, X + ("y",), 0, 0, tiled=True)
    return jnp.sum(blocks.astype(jnp.float32), axis=0)


def gradient_kernel(cotangent_ref, inputs_ref, out_ref):
    terms = jnp.dot(cotangent_ref[...], inputs_ref[...], preferred_element_type=jnp.float32)
    out_ref[...] = terms.astype(out_ref.dtype).reshape(out_ref.shape)


def gradient_terms(cotangent, inputs):
    tokens, depth = inputs.shape
    part = cotangent.shape[0] // 16
    return pl.pallas_call(
        gradient_kernel,
        grid=(4,),
        in_specs=[
            pl.BlockSpec((4 * part, tokens), lambda i: (i, 0)),
            pl.BlockSpec((tokens, depth), lambda i: (0, 0)),
        ],
        out_specs=pl.BlockSpec((4, 1, part, depth), lambda i: (i % 2, i // 2, 0, 0)),
        out_shape=jax.ShapeDtypeStruct((8, 2, part, depth), jnp.bfloat16),
        compiler_params=pltpu.CompilerParams(vmem_limit_bytes=60 * 1024 * 1024),
        cost_estimate=pl.CostEstimate(
            flops=2 * 16 * part * tokens * depth, bytes_accessed=17_000_000, transcendentals=0
        ),
    )(cotangent, inputs)


def project_block(weight, attended, out_ref, n):
    dims = (((1,), (1,)), ((), ()))
    total = lax.dot_general(weight[0], attended[0], dims, preferred_element_type=jnp.float32)
    total += lax.dot_general(weight[1], attended[1], dims, preferred_element_type=jnp.float32)
    out_ref[n] = total.astype(out_ref.dtype)


def project_all_kernel(weight_ref, tokens_ref, out_ref):
    for n in range(8):
        project_block(weight_ref, tokens_ref.at[n % 4, :, n // 4], out_ref, n)


def project_all(weight, attended):
    part, depth = weight.shape[1:]
    tokens = attended.shape[3]
    return pl.pallas_call(
        project_all_kernel,
        out_shape=jax.ShapeDtypeStruct((8, part, tokens), jnp.bfloat16),
        compiler_params=pltpu.CompilerParams(vmem_limit_bytes=32 * 1024 * 1024),
        cost_estimate=pl.CostEstimate(
            flops=32 * part * depth * tokens, bytes_accessed=3_000_000, transcendentals=0
        ),
    )(weight, attended)


def project_own_kernel(weight_ref, tokens_ref, out_ref):
    project_block(weight_ref.at[0], tokens_ref.at[:, 0], out_ref.at[0], 0)


def project_own(weight, attended):
    part, depth = weight.shape[2:]
    tokens = attended.shape[2]
    out = pl.pallas_call(
        project_own_kernel,
        grid=(2, 4),
        in_specs=[
            pl.BlockSpec((1, 2, part, depth), lambda r, k: (k, 0, 0, 0)),
            pl.BlockSpec((2, 1, tokens, depth), lambda r, k: (0, r, 0, 0)),
        ],
        out_specs=pl.BlockSpec((1, 1, part, tokens), lambda r, k: (r, k, 0, 0)),
        out_shape=jax.ShapeDtypeStruct((2, 4, part, tokens), jnp.bfloat16),
        compiler_params=pltpu.CompilerParams(vmem_limit_bytes=32 * 1024 * 1024),
        cost_estimate=pl.CostEstimate(
            flops=32 * part * depth * tokens, bytes_accessed=4_000_000, transcendentals=0
        ),
    )(weight, attended)
    return out.reshape(8, part, tokens)


def normalize(state, norm_gain):
    values = state.astype(jnp.float32)
    mean_square = jnp.mean(values * values, axis=0, keepdims=True)
    return (values * lax.rsqrt(mean_square + NORM_EPS) * norm_gain[:, None]).astype(jnp.bfloat16)


def piece_products(piece, gain, weight):
    values = piece.astype(jnp.float32)
    squares = jnp.sum(values * values, axis=(0, 1))
    scaled = (values * gain[..., None]).astype(jnp.bfloat16).reshape(-1, piece.shape[-1])
    dims = (((0,), (0,)), ((), ()))
    return squares, lax.dot_general(scaled, weight, dims, preferred_element_type=jnp.float32)


def revise(current_state, update, pick_codes, mask_values):
    values = current_state.astype(jnp.float32)
    masked = jnp.broadcast_to(mask_values.astype(jnp.float32)[..., None], values.shape)
    return jnp.where(
        pick_codes == 1, values + update, jnp.where(pick_codes == 2, masked, values)
    ).astype(jnp.bfloat16)


def attend(queries, cache_keys, cache_values, block_keys, block_values, prefix_lengths):
    score_scale = HEAD ** (-0.5)
    prefix_len = cache_keys.shape[1]
    prefix_scores = (
        jnp.einsum("rbgh,rph->rgbp", queries, cache_keys, preferred_element_type=jnp.float32)
        * score_scale
    )
    valid_keys = jnp.arange(prefix_len, dtype=jnp.int32)[None, :] < prefix_lengths[:, None]
    prefix_scores = jnp.where(valid_keys[:, None, None, :], prefix_scores, -jnp.inf)
    block_scores = (
        jnp.einsum("rbgh,rch->rgbc", queries, block_keys, preferred_element_type=jnp.float32)
        * score_scale
    )
    score_top = jnp.maximum(jnp.max(prefix_scores, axis=-1), jnp.max(block_scores, axis=-1))[
        ..., None
    ]
    prefix_exp = jnp.exp(prefix_scores - score_top)
    block_exp = jnp.exp(block_scores - score_top)
    denom_sum = (jnp.sum(prefix_exp, axis=-1) + jnp.sum(block_exp, axis=-1))[..., None]
    prefix_probs = (prefix_exp / denom_sum).astype(jnp.bfloat16)
    block_probs = (block_exp / denom_sum).astype(jnp.bfloat16)
    attended = jnp.einsum(
        "rgbp,rph->rbgh", prefix_probs, cache_values, preferred_element_type=jnp.float32
    )
    attended = attended + jnp.einsum(
        "rgbc,rch->rbgh", block_probs, block_values, preferred_element_type=jnp.float32
    )
    return attended.astype(jnp.bfloat16).reshape(queries.shape[0] * queries.shape[1], -1)


def on_device(
    learner_inputs,
    learner_cotangent,
    master_weight,
    first_moment,
    second_moment,
    query_weight,
    keyval_weight,
    prefix_cache,
    block_states,
    norm_gain,
    mask_vector,
    prefix_lengths,
    position_picks,
):
    bf16, f32 = jnp.bfloat16, jnp.float32
    role, core, dp = lax.axis_index("role"), lax.axis_index("core"), lax.axis_index("dp")
    row_count, block_len, part = block_states.shape
    tokens = row_count * block_len
    depth = learner_inputs.shape[1]
    out_scale = (HEADS * HEAD) ** (-0.5)

    cache_other = rotate(prefix_cache, "core", 1)
    cache_keys = jnp.where(core == 0, prefix_cache, cache_other)
    cache_values = jnp.where(core == 0, cache_other, prefix_cache)

    ix, iy = lax.axis_index(X), lax.axis_index("y")

    def half_of(array, which):
        blocks = array.reshape((4, 2, 2, part) + array.shape[1:])
        return lax.dynamic_index_in_dim(blocks, which, 2, keepdims=False)

    masks = half_of(mask_vector, core)

    def attended_from(queries, own_half):
        other_half = rotate(own_half, "core", 1)
        block_keys = jnp.where(core == 0, own_half, other_half).reshape(row_count, block_len, HEAD)
        block_values = jnp.where(core == 0, other_half, own_half).reshape(
            row_count, block_len, HEAD
        )
        return attend(
            queries.reshape(row_count, block_len, -1, HEAD),
            cache_keys,
            cache_values,
            block_keys,
            block_values,
            prefix_lengths,
        )

    def product(normed, weight):
        return lax.dot_general(
            normed, weight, (((0,), (0,)), ((), ())), preferred_element_type=f32
        ).astype(bf16)

    cotangent = lax.all_gather(learner_cotangent, TENSOR, axis=1, tiled=True)
    state = block_states.reshape(tokens, part).T
    square, whole = gather_rows(pair_order(state, rotate(state, "y", 1), iy, 0))
    normed = normalize(whole.reshape(-1, tokens), norm_gain)
    attended = attended_from(product(normed, query_weight), product(normed, keyval_weight))
    both = jnp.stack([swap_cores(attended), swap_cores(attended, True)])
    attended_all, cotangent = gather_ring(both, cotangent)

    terms = gradient_terms(cotangent.T, learner_inputs)
    halves = lax.psum_scatter(terms, "dp", scatter_dimension=0, tiled=False)
    shift_x, shift_y = role * 2 + dp // 4, dp // 2 % 2
    joined = jnp.concatenate([query_weight, keyval_weight], 1)
    sides = []
    for which in (core, 1 - core):
        gains, weights = half_of(norm_gain, which), half_of(joined, which)
        for turn in range(4):
            index = ix ^ shift_x ^ turn
            sides.append((pick(gains, index), pick(weights, index).reshape(-1, joined.shape[1])))
    halves, attended_all, sides = lax.optimization_barrier((halves, attended_all, sides))
    gradient = pick(halves, role).astype(f32) + rotate(pick(halves, 1 - role), "role", 1).astype(f32)
    new_weight, new_first, new_second = adam_update(
        gradient, master_weight.T, first_moment.T, second_moment.T
    )
    weight_part = new_weight.astype(bf16)
    weight_pair = pair_order(weight_part, rotate(weight_part, "core", 1), core, 0)

    partial = project_all(weight_pair, attended_all.reshape(4, 2, 2, tokens, depth))
    weight_half, partial = lax.optimization_barrier((swap_cores(weight_part), partial))
    weight_all = lax.all_gather(weight_half, "dp", axis=0)
    update = scatter_sum(partial).astype(bf16)

    def deal(flip):
        route = []
        for source in range(256):
            r, d2, d1, d0, x1, x0, y, c = [source >> k & 1 for k in range(7, -1, -1)]
            target = [r ^ x1, d2 ^ x0, d1 ^ y, c, x1, x0, y ^ flip, d0]
            route.append((source, sum(bit << 7 - k for k, bit in enumerate(target))))
        return lax.ppermute(update, EVERY, route)

    update = pair_order(deal(0), deal(1), iy ^ shift_y, 0).astype(f32) * out_scale
    picks = position_picks.reshape(STEPS, 1, tokens)
    rows = revise(pick(square, ix ^ shift_x), update, picks[0], pick(masks, ix ^ shift_x))

    pieces = [rows]
    for turn in range(1, 4):
        pieces.append(lax.ppermute(rows, X, [(x, x ^ turn) for x in range(4)]))
    crossed = [rotate(piece, "core", 1) for piece in pieces]
    squares, products = 0.0, 0.0
    for piece, side in zip(pieces + crossed, sides):
        more_squares, more_products = piece_products(piece, *side)
        squares, products = squares + more_squares, products + more_products
    factor = lax.rsqrt(squares / (16 * part) + NORM_EPS)[:, None]
    products = (products * factor).astype(bf16)
    products, weight_all = lax.optimization_barrier((products, weight_all))
    attended = attended_from(products[:, :depth], products[:, depth:])
    attended_pair = pair_order(attended, rotate(attended, "core", 1), core, 0)
    route = [(r * 2 + c, (1 - r) * 2 + 1 - c) for r in range(2) for c in range(2)]
    far = lax.ppermute(attended, ("role", "core"), route)
    far_pair = pair_order(rotate(attended, "role", 1), far, core, 0)
    attended_four = pair_order(attended_pair, far_pair, role, 1)
    partial = project_own(weight_all.reshape(4, 2, part, depth), attended_four)
    update = scatter_sum(partial).astype(bf16)
    update = lax.ppermute(update, ("role", "x1"), [(0, 0), (1, 2), (2, 1), (3, 3)])
    state = pick(pick(jnp.stack(pieces), shift_x), iy)
    state = revise(state, update.astype(f32) * out_scale, picks[1], pick(pick(masks, ix), iy))
    return (state.T.reshape(row_count, block_len, part), new_weight.T, new_first.T, new_second.T)


def solution(mesh):
    fine = Mesh(mesh.devices.reshape(2, 8, 2, 2, 2, 2), EVERY)
    weights = P(TENSOR, RD)
    return jax.shard_map(
        on_device,
        mesh=fine,
        in_specs=(
            P(RD, TENSOR),
            P(RD, TENSOR),
            weights,
            weights,
            weights,
            P(None, TENSOR),
            P(None, TENSOR),
            P(RD, None, TENSOR),
            P(RD, None, TENSOR),
            P(),
            P(),
            P(RD),
            P(None, RD, None),
        ),
        out_specs=(P(RD, None, TENSOR), weights, weights, weights),
        check_vma=False,
    )
```

```python
import jax
import jax.numpy as jnp
from jax import lax
from jax.experimental import pallas as pl
from jax.experimental.pallas import tpu as pltpu
from jax.sharding import Mesh, PartitionSpec as P

HEADS = 64
HEAD = 128
STEPS = 2

BETA_ONE = 0.9
BETA_TWO = 0.95
ADAM_EPS = 1e-08
LEARN_RATE = 0.5
DECAY_RATE = 0.1
STEP_COUNT = 50
NORM_EPS = 1e-06

RD = ("role", "dp")
X = ("x1", "x0")
TENSOR = X + ("y", "core")
EVERY = RD + TENSOR


def rotate(block, axis, shift):
    count = 4 if axis == X else lax.axis_size(axis)
    return lax.ppermute(block, axis, [(low, (low + shift) % count) for low in range(count)])


def pick(blocks, index):
    return lax.dynamic_index_in_dim(blocks, index, 0, keepdims=False)


def pair_order(own, other, index, axis):
    return jnp.where(index == 0, jnp.stack([own, other], axis), jnp.stack([other, own], axis))


def adam_update(gradient, master_weight, first_moment, second_moment):
    first_new = BETA_ONE * first_moment + (1.0 - BETA_ONE) * gradient
    second_new = BETA_TWO * second_moment + (1.0 - BETA_TWO) * gradient * gradient
    first_hat = first_new / (1.0 - BETA_ONE**STEP_COUNT)
    second_hat = second_new / (1.0 - BETA_TWO**STEP_COUNT)
    weight_new = master_weight - LEARN_RATE * (
        first_hat / (jnp.sqrt(second_hat) + ADAM_EPS) + DECAY_RATE * master_weight
    )
    return (weight_new, first_new, second_new)


def gather_rows(rows, shift_x, beside=None):
    ix, ic = lax.axis_index(X), lax.axis_index("core")
    ahead, back, across = rotate(rows, X, 1), rotate(rows, X, -1), rotate(rows, X, 2)
    square = jnp.zeros((4,) + rows.shape, rows.dtype)
    square = lax.dynamic_update_index_in_dim(square, rows, ix ^ shift_x, 0)
    square = lax.dynamic_update_index_in_dim(square, ahead, ((ix + 3) % 4) ^ shift_x, 0)
    square = lax.dynamic_update_index_in_dim(square, back, ((ix + 1) % 4) ^ shift_x, 0)
    square = lax.dynamic_update_index_in_dim(square, across, ((ix + 2) % 4) ^ shift_x, 0)
    other, beside = lax.optimization_barrier((rotate(square, "core", 1), beside))
    return pair_order(square, other, ic, 2), beside


def swap_cores(block, flip_role=False):
    route = []
    for role in range(2):
        for dp in range(8):
            for core in range(2):
                low = dp % 2
                source = (role * 8 + dp) * 2 + core
                target_role = 1 - role if flip_role else role
                target = (target_role * 8 + dp - low + core) * 2 + low
                route.append((source, target))
    return lax.ppermute(block, ("role", "dp", "core"), route)


def gather_ring(block, before):
    me = lax.axis_index("dp")
    high = me - me % 2
    up, down = [block], [block]
    for step in range(3):
        up.append(rotate(up[-1], "dp", 1))
        down.append(rotate(down[-1], "dp", -1))
    before, up, down = lax.optimization_barrier((before, up, down))
    up.append(rotate(up[-1], "dp", 1))
    whole = jnp.zeros((8,) + block.shape, block.dtype)
    for step in range(5):
        whole = lax.dynamic_update_index_in_dim(whole, up[step], ((me + 8 - step) % 8) ^ high, 0)
    for step in range(1, 4):
        whole = lax.dynamic_update_index_in_dim(whole, down[step], ((me + step) % 8) ^ high, 0)
    return whole, before


def scatter_sum(parts):
    blocks = lax.all_to_all(parts, X + ("y",), 0, 0, tiled=True)
    return jnp.sum(blocks.astype(jnp.float32), axis=0)


def gradient_kernel(cotangent_ref, inputs_ref, out_ref):
    terms = jnp.dot(cotangent_ref[...], inputs_ref[...], preferred_element_type=jnp.float32)
    out_ref[...] = terms.astype(out_ref.dtype).reshape(out_ref.shape)


def gradient_terms(cotangent, inputs):
    tokens, depth = inputs.shape
    part = cotangent.shape[0] // 16
    return pl.pallas_call(
        gradient_kernel,
        grid=(4,),
        in_specs=[
            pl.BlockSpec((4 * part, tokens), lambda i: (i, 0)),
            pl.BlockSpec((tokens, depth), lambda i: (0, 0)),
        ],
        out_specs=pl.BlockSpec((4, 1, part, depth), lambda i: (i % 2, i // 2, 0, 0)),
        out_shape=jax.ShapeDtypeStruct((8, 2, part, depth), jnp.bfloat16),
        compiler_params=pltpu.CompilerParams(vmem_limit_bytes=60 * 1024 * 1024),
        cost_estimate=pl.CostEstimate(
            flops=2 * 16 * part * tokens * depth, bytes_accessed=17_000_000, transcendentals=0
        ),
    )(cotangent, inputs)


def contract(weights, tokens):
    dims = (((1,), (1,)), ((), ()))
    total = 0.0
    for weight, values in zip(weights, tokens):
        total += lax.dot_general(weight, values, dims, preferred_element_type=jnp.float32)
    return total.astype(jnp.bfloat16)


def project_all_kernel(place_ref, own_ref, other_ref, tokens_ref, out_ref):
    core = place_ref[1]
    weights = own_ref[...], other_ref[...]
    for n in range(8):
        tokens = [tokens_ref[n % 4, half, n // 4] for half in (core, 1 - core)]
        out_ref[n] = contract(weights, tokens)


def project_all(place, own, other, attended):
    part, depth = own.shape
    tokens = attended.shape[3]
    vmem = pl.BlockSpec(memory_space=pltpu.VMEM)
    return pl.pallas_call(
        project_all_kernel,
        in_specs=[pl.BlockSpec(memory_space=pltpu.SMEM), vmem, vmem, vmem],
        out_specs=vmem,
        out_shape=jax.ShapeDtypeStruct((8, part, tokens), jnp.bfloat16),
        compiler_params=pltpu.CompilerParams(vmem_limit_bytes=32 * 1024 * 1024),
        cost_estimate=pl.CostEstimate(
            flops=32 * part * depth * tokens, bytes_accessed=3_000_000, transcendentals=0
        ),
    )(place, own, other, attended)


def project_own_kernel(place_ref, weight_ref, own_ref, other_ref, far_own_ref, far_other_ref, out_ref):
    role, core = place_ref[0], place_ref[1]
    weights = weight_ref[0, core], weight_ref[0, 1 - core]
    out_ref[role, 0] = contract(weights, (own_ref[...], other_ref[...]))
    out_ref[1 - role, 0] = contract(weights, (far_own_ref[...], far_other_ref[...]))


def project_own(place, weight, *attended):
    part, depth = weight.shape[2:]
    tokens = attended[0].shape[0]
    whole = pl.BlockSpec((tokens, depth), lambda k: (0, 0))
    out = pl.pallas_call(
        project_own_kernel,
        grid=(4,),
        in_specs=[
            pl.BlockSpec(memory_space=pltpu.SMEM),
            pl.BlockSpec((1, 2, part, depth), lambda k: (k, 0, 0, 0)),
            whole,
            whole,
            whole,
            whole,
        ],
        out_specs=pl.BlockSpec((2, 1, part, tokens), lambda k: (0, k, 0, 0)),
        out_shape=jax.ShapeDtypeStruct((2, 4, part, tokens), jnp.bfloat16),
        compiler_params=pltpu.CompilerParams(vmem_limit_bytes=32 * 1024 * 1024),
        cost_estimate=pl.CostEstimate(
            flops=32 * part * depth * tokens, bytes_accessed=4_000_000, transcendentals=0
        ),
    )(place, weight, *attended)
    return out.reshape(8, part, tokens)


def normalize(state, norm_gain):
    values = state.astype(jnp.float32)
    mean_square = jnp.mean(values * values, axis=0, keepdims=True)
    return (values * lax.rsqrt(mean_square + NORM_EPS) * norm_gain[:, None]).astype(jnp.bfloat16)


def revise(current_state, update, pick_codes, mask_values):
    values = current_state.astype(jnp.float32)
    masked = jnp.broadcast_to(mask_values.astype(jnp.float32)[..., None], values.shape)
    return jnp.where(
        pick_codes == 1, values + update, jnp.where(pick_codes == 2, masked, values)
    ).astype(jnp.bfloat16)


def attend(queries, cache_keys, cache_values, block_keys, block_values, prefix_lengths):
    score_scale = HEAD ** (-0.5)
    prefix_len = cache_keys.shape[1]
    prefix_scores = (
        jnp.einsum("rbgh,rph->rgbp", queries, cache_keys, preferred_element_type=jnp.float32)
        * score_scale
    )
    valid_keys = jnp.arange(prefix_len, dtype=jnp.int32)[None, :] < prefix_lengths[:, None]
    prefix_scores = jnp.where(valid_keys[:, None, None, :], prefix_scores, -jnp.inf)
    block_scores = (
        jnp.einsum("rbgh,rch->rgbc", queries, block_keys, preferred_element_type=jnp.float32)
        * score_scale
    )
    score_top = jnp.maximum(jnp.max(prefix_scores, axis=-1), jnp.max(block_scores, axis=-1))[
        ..., None
    ]
    prefix_exp = jnp.exp(prefix_scores - score_top)
    block_exp = jnp.exp(block_scores - score_top)
    denom_sum = (jnp.sum(prefix_exp, axis=-1) + jnp.sum(block_exp, axis=-1))[..., None]
    prefix_probs = (prefix_exp / denom_sum).astype(jnp.bfloat16)
    block_probs = (block_exp / denom_sum).astype(jnp.bfloat16)
    attended = jnp.einsum(
        "rgbp,rph->rbgh", prefix_probs, cache_values, preferred_element_type=jnp.float32
    )
    attended = attended + jnp.einsum(
        "rgbc,rch->rbgh", block_probs, block_values, preferred_element_type=jnp.float32
    )
    return attended.astype(jnp.bfloat16).reshape(queries.shape[0] * queries.shape[1], -1)


def on_device(
    learner_inputs,
    learner_cotangent,
    master_weight,
    first_moment,
    second_moment,
    query_weight,
    keyval_weight,
    prefix_cache,
    block_states,
    norm_gain,
    mask_vector,
    prefix_lengths,
    position_picks,
):
    bf16, f32 = jnp.bfloat16, jnp.float32
    role, core, dp = lax.axis_index("role"), lax.axis_index("core"), lax.axis_index("dp")
    row_count, block_len, part = block_states.shape
    tokens = row_count * block_len
    depth = learner_inputs.shape[1]
    out_scale = (HEADS * HEAD) ** (-0.5)

    cache_other = rotate(prefix_cache, "core", 1)
    cache_keys = jnp.where(core == 0, prefix_cache, cache_other)
    cache_values = jnp.where(core == 0, cache_other, prefix_cache)

    masks = mask_vector.reshape(4, 2, 2, part)
    ix, iy = lax.axis_index(X), lax.axis_index("y")

    def rows_of(blocks, index):
        return lax.dynamic_index_in_dim(pick(blocks, index), core, 1, keepdims=False)

    def attended_of(whole):
        normed = normalize(whole.reshape(-1, tokens), norm_gain)
        own_half = lax.dot_general(
            normed, keyval_weight, (((0,), (0,)), ((), ())), preferred_element_type=f32
        ).astype(bf16)
        other_half = rotate(own_half, "core", 1)
        queries = lax.dot_general(
            normed, query_weight, (((0,), (0,)), ((), ())), preferred_element_type=f32
        ).astype(bf16)
        block_keys = jnp.where(core == 0, own_half, other_half).reshape(row_count, block_len, HEAD)
        block_values = jnp.where(core == 0, other_half, own_half).reshape(row_count, block_len, HEAD)
        return attend(
            queries.reshape(row_count, block_len, -1, HEAD),
            cache_keys,
            cache_values,
            block_keys,
            block_values,
            prefix_lengths,
        )

    cotangent = lax.all_gather(learner_cotangent, TENSOR, axis=1, tiled=True)
    state = block_states.reshape(tokens, part).T
    whole, _ = gather_rows(pair_order(state, rotate(state, "y", 1), iy, 0), 0)
    attended = attended_of(whole)
    both = jnp.stack([swap_cores(attended), swap_cores(attended, True)])
    attended_all, cotangent = gather_ring(both, cotangent)

    terms = gradient_terms(cotangent.T, learner_inputs)
    halves = lax.psum_scatter(terms, "dp", scatter_dimension=0, tiled=False)
    halves, attended_all = lax.optimization_barrier((halves, attended_all))
    gradient = pick(halves, role).astype(f32) + rotate(pick(halves, 1 - role), "role", 1).astype(f32)
    new_weight, new_first, new_second = adam_update(
        gradient, master_weight.T, first_moment.T, second_moment.T
    )
    weight_part = new_weight.astype(bf16)

    place = jnp.stack([role, core]).astype(jnp.int32)
    partial = project_all(
        place,
        weight_part,
        rotate(weight_part, "core", 1),
        attended_all.reshape(4, 2, 2, tokens, depth),
    )
    weight_half, partial = lax.optimization_barrier((swap_cores(weight_part), partial))
    weight_all = lax.all_gather(weight_half, "dp", axis=0)
    update = scatter_sum(partial).astype(bf16)

    def deal(flip):
        route = []
        for source in range(256):
            r, d2, d1, d0, x1, x0, y, c = [source >> k & 1 for k in range(7, -1, -1)]
            target = [r ^ x1, d2 ^ x0, d1 ^ y, c, x1, x0, y ^ flip, d0]
            route.append((source, sum(bit << 7 - k for k, bit in enumerate(target))))
        return lax.ppermute(update, EVERY, route)

    shift_x, shift_y = role * 2 + dp // 4, dp // 2 % 2
    update = pair_order(deal(0), deal(1), iy ^ shift_y, 0).astype(f32) * out_scale
    picks = position_picks.reshape(STEPS, 1, tokens)
    rows = revise(rows_of(whole, ix ^ shift_x), update, picks[0], rows_of(masks, ix ^ shift_x))

    whole, weight_all = gather_rows(rows, shift_x, weight_all)
    attended = attended_of(whole)
    route = [(r * 2 + c, (1 - r) * 2 + 1 - c) for r in range(2) for c in range(2)]
    partial = project_own(
        place,
        weight_all.reshape(4, 2, part, depth),
        attended,
        rotate(attended, "core", 1),
        rotate(attended, "role", 1),
        lax.ppermute(attended, ("role", "core"), route),
    )
    update = scatter_sum(partial).astype(bf16)
    update = lax.ppermute(update, ("role", "x1"), [(0, 0), (1, 2), (2, 1), (3, 3)])
    state = pick(rows_of(whole, ix), iy)
    state = revise(state, update.astype(f32) * out_scale, picks[1], pick(rows_of(masks, ix), iy))
    return (state.T.reshape(row_count, block_len, part), new_weight.T, new_first.T, new_second.T)


def solution(mesh):
    fine = Mesh(mesh.devices.reshape(2, 8, 2, 2, 2, 2), EVERY)
    weights = P(TENSOR, RD)
    return jax.shard_map(
        on_device,
        mesh=fine,
        in_specs=(
            P(RD, TENSOR),
            P(RD, TENSOR),
            weights,
            weights,
            weights,
            P(None, TENSOR),
            P(None, TENSOR),
            P(RD, None, TENSOR),
            P(RD, None, TENSOR),
            P(),
            P(),
            P(RD),
            P(None, RD, None),
        ),
        out_specs=(P(RD, None, TENSOR), weights, weights, weights),
        check_vma=False,
    )
```

```python
import jax
import jax.numpy as jnp
from jax import lax
from jax.experimental import pallas as pl
from jax.experimental.pallas import tpu as pltpu
from jax.sharding import Mesh, PartitionSpec as P

HEADS = 64
HEAD = 128
STEPS = 2

BETA_ONE = 0.9
BETA_TWO = 0.95
ADAM_EPS = 1e-08
LEARN_RATE = 0.5
DECAY_RATE = 0.1
STEP_COUNT = 50
NORM_EPS = 1e-06

RD = ("role", "dp")
X = ("x1", "x0")
TENSOR = X + ("y", "core")
EVERY = RD + TENSOR


def rotate(block, axis, shift):
    count = 4 if axis == X else lax.axis_size(axis)
    return lax.ppermute(block, axis, [(low, (low + shift) % count) for low in range(count)])


def pick(blocks, index):
    return lax.dynamic_index_in_dim(blocks, index, 0, keepdims=False)


def pair_order(own, other, index, axis):
    return jnp.where(index == 0, jnp.stack([own, other], axis), jnp.stack([other, own], axis))


def adam_update(gradient, master_weight, first_moment, second_moment):
    first_new = BETA_ONE * first_moment + (1.0 - BETA_ONE) * gradient
    second_new = BETA_TWO * second_moment + (1.0 - BETA_TWO) * gradient * gradient
    first_hat = first_new / (1.0 - BETA_ONE**STEP_COUNT)
    second_hat = second_new / (1.0 - BETA_TWO**STEP_COUNT)
    weight_new = master_weight - LEARN_RATE * (
        first_hat / (jnp.sqrt(second_hat) + ADAM_EPS) + DECAY_RATE * master_weight
    )
    return (weight_new, first_new, second_new)


def gather_rows(rows, shift_x, beside=None):
    ix, ic = lax.axis_index(X), lax.axis_index("core")
    ahead, back, across = rotate(rows, X, 1), rotate(rows, X, -1), rotate(rows, X, 2)
    square = jnp.zeros((4,) + rows.shape, rows.dtype)
    square = lax.dynamic_update_index_in_dim(square, rows, ix ^ shift_x, 0)
    square = lax.dynamic_update_index_in_dim(square, ahead, ((ix + 3) % 4) ^ shift_x, 0)
    square = lax.dynamic_update_index_in_dim(square, back, ((ix + 1) % 4) ^ shift_x, 0)
    square = lax.dynamic_update_index_in_dim(square, across, ((ix + 2) % 4) ^ shift_x, 0)
    other, beside = lax.optimization_barrier((rotate(square, "core", 1), beside))
    return pair_order(square, other, ic, 2), beside


def swap_cores(block, flip_role=False):
    route = []
    for role in range(2):
        for dp in range(8):
            for core in range(2):
                low = dp % 2
                source = (role * 8 + dp) * 2 + core
                target_role = 1 - role if flip_role else role
                target = (target_role * 8 + dp - low + core) * 2 + low
                route.append((source, target))
    return lax.ppermute(block, ("role", "dp", "core"), route)


def gather_ring(block, before):
    me = lax.axis_index("dp")
    high = me - me % 2
    up, down = [block], [block]
    for step in range(3):
        up.append(rotate(up[-1], "dp", 1))
        down.append(rotate(down[-1], "dp", -1))
    before, up, down = lax.optimization_barrier((before, up, down))
    up.append(rotate(up[-1], "dp", 1))
    whole = jnp.zeros((8,) + block.shape, block.dtype)
    for step in range(5):
        whole = lax.dynamic_update_index_in_dim(whole, up[step], ((me + 8 - step) % 8) ^ high, 0)
    for step in range(1, 4):
        whole = lax.dynamic_update_index_in_dim(whole, down[step], ((me + step) % 8) ^ high, 0)
    return whole, before


def scatter_sum(parts):
    blocks = lax.all_to_all(parts, X + ("y",), 0, 0, tiled=True)
    return jnp.sum(blocks.astype(jnp.float32), axis=0)


def gradient_kernel(cotangent_ref, inputs_ref, out_ref):
    terms = jnp.dot(cotangent_ref[...], inputs_ref[...], preferred_element_type=jnp.float32)
    out_ref[...] = terms.astype(out_ref.dtype).reshape(out_ref.shape)


def gradient_terms(cotangent, inputs):
    tokens, depth = inputs.shape
    part = cotangent.shape[0] // 16
    return pl.pallas_call(
        gradient_kernel,
        grid=(4,),
        in_specs=[
            pl.BlockSpec((4 * part, tokens), lambda i: (i, 0)),
            pl.BlockSpec((tokens, depth), lambda i: (0, 0)),
        ],
        out_specs=pl.BlockSpec((4, 1, part, depth), lambda i: (i % 2, i // 2, 0, 0)),
        out_shape=jax.ShapeDtypeStruct((8, 2, part, depth), jnp.bfloat16),
        compiler_params=pltpu.CompilerParams(vmem_limit_bytes=60 * 1024 * 1024),
        cost_estimate=pl.CostEstimate(
            flops=2 * 16 * part * tokens * depth, bytes_accessed=17_000_000, transcendentals=0
        ),
    )(cotangent, inputs)


def contract(weights, tokens):
    dims = (((1,), (1,)), ((), ()))
    total = 0.0
    for weight, values in zip(weights, tokens):
        total += lax.dot_general(weight, values, dims, preferred_element_type=jnp.float32)
    return total.astype(jnp.bfloat16)


def project_all_kernel(place_ref, own_ref, other_ref, tokens_ref, out_ref):
    core = place_ref[1]
    weights = own_ref[...], other_ref[...]
    for n in range(8):
        tokens = [tokens_ref[n % 4, half, n // 4] for half in (core, 1 - core)]
        out_ref[n] = contract(weights, tokens)


def project_all(place, own, other, attended):
    part, depth = own.shape
    tokens = attended.shape[3]
    vmem = pl.BlockSpec(memory_space=pltpu.VMEM)
    return pl.pallas_call(
        project_all_kernel,
        in_specs=[pl.BlockSpec(memory_space=pltpu.SMEM), vmem, vmem, vmem],
        out_specs=vmem,
        out_shape=jax.ShapeDtypeStruct((8, part, tokens), jnp.bfloat16),
        compiler_params=pltpu.CompilerParams(vmem_limit_bytes=32 * 1024 * 1024),
        cost_estimate=pl.CostEstimate(
            flops=32 * part * depth * tokens, bytes_accessed=3_000_000, transcendentals=0
        ),
    )(place, own, other, attended)


def project_own_kernel(place_ref, weight_ref, own_ref, far_ref, near_ref, away_ref):
    role, core = place_ref[0], place_ref[1]
    dims = (((1,), (1,)), ((), ()))
    for tokens_ref, index in ((own_ref, role), (far_ref, 1 - role)):
        tokens = tokens_ref[...]
        near_ref[index, 0] = lax.dot_general(
            weight_ref[core], tokens, dims, preferred_element_type=jnp.float32
        )
        away_ref[index, 0] = contract((weight_ref[1 - core],), (tokens,))


def project_own(place, weight, own, far):
    part, depth = weight.shape[1:]
    tokens = own.shape[0]
    whole = pl.BlockSpec((tokens, depth), lambda k: (0, 0))
    block = pl.BlockSpec((2, 1, part, tokens), lambda k: (0, k, 0, 0))
    return pl.pallas_call(
        project_own_kernel,
        grid=(4,),
        in_specs=[
            pl.BlockSpec(memory_space=pltpu.SMEM),
            pl.BlockSpec((2, part, depth), lambda k: (k, 0, 0)),
            whole,
            whole,
        ],
        out_specs=[block, block],
        out_shape=[
            jax.ShapeDtypeStruct((2, 4, part, tokens), jnp.float32),
            jax.ShapeDtypeStruct((2, 4, part, tokens), jnp.bfloat16),
        ],
        compiler_params=pltpu.CompilerParams(vmem_limit_bytes=32 * 1024 * 1024),
        cost_estimate=pl.CostEstimate(
            flops=32 * part * depth * tokens, bytes_accessed=5_000_000, transcendentals=0
        ),
    )(place, weight, own, far)


def normalize(state, norm_gain):
    values = state.astype(jnp.float32)
    mean_square = jnp.mean(values * values, axis=0, keepdims=True)
    return (values * lax.rsqrt(mean_square + NORM_EPS) * norm_gain[:, None]).astype(jnp.bfloat16)


def revise(current_state, update, pick_codes, mask_values):
    values = current_state.astype(jnp.float32)
    masked = jnp.broadcast_to(mask_values.astype(jnp.float32)[..., None], values.shape)
    return jnp.where(
        pick_codes == 1, values + update, jnp.where(pick_codes == 2, masked, values)
    ).astype(jnp.bfloat16)


def attend(queries, cache_keys, cache_values, block_keys, block_values, prefix_lengths):
    score_scale = HEAD ** (-0.5)
    prefix_len = cache_keys.shape[1]
    prefix_scores = (
        jnp.einsum("rbgh,rph->rgbp", queries, cache_keys, preferred_element_type=jnp.float32)
        * score_scale
    )
    valid_keys = jnp.arange(prefix_len, dtype=jnp.int32)[None, :] < prefix_lengths[:, None]
    prefix_scores = jnp.where(valid_keys[:, None, None, :], prefix_scores, -jnp.inf)
    block_scores = (
        jnp.einsum("rbgh,rch->rgbc", queries, block_keys, preferred_element_type=jnp.float32)
        * score_scale
    )
    score_top = jnp.maximum(jnp.max(prefix_scores, axis=-1), jnp.max(block_scores, axis=-1))[
        ..., None
    ]
    prefix_exp = jnp.exp(prefix_scores - score_top)
    block_exp = jnp.exp(block_scores - score_top)
    denom_sum = (jnp.sum(prefix_exp, axis=-1) + jnp.sum(block_exp, axis=-1))[..., None]
    prefix_probs = (prefix_exp / denom_sum).astype(jnp.bfloat16)
    block_probs = (block_exp / denom_sum).astype(jnp.bfloat16)
    attended = jnp.einsum(
        "rgbp,rph->rbgh", prefix_probs, cache_values, preferred_element_type=jnp.float32
    )
    attended = attended + jnp.einsum(
        "rgbc,rch->rbgh", block_probs, block_values, preferred_element_type=jnp.float32
    )
    return attended.astype(jnp.bfloat16).reshape(queries.shape[0] * queries.shape[1], -1)


def on_device(
    learner_inputs,
    learner_cotangent,
    master_weight,
    first_moment,
    second_moment,
    query_weight,
    keyval_weight,
    prefix_cache,
    block_states,
    norm_gain,
    mask_vector,
    prefix_lengths,
    position_picks,
):
    bf16, f32 = jnp.bfloat16, jnp.float32
    role, core, dp = lax.axis_index("role"), lax.axis_index("core"), lax.axis_index("dp")
    row_count, block_len, part = block_states.shape
    tokens = row_count * block_len
    depth = learner_inputs.shape[1]
    out_scale = (HEADS * HEAD) ** (-0.5)

    cache_other = rotate(prefix_cache, "core", 1)
    cache_keys = jnp.where(core == 0, prefix_cache, cache_other)
    cache_values = jnp.where(core == 0, cache_other, prefix_cache)

    masks = mask_vector.reshape(4, 2, 2, part)
    ix, iy = lax.axis_index(X), lax.axis_index("y")

    def rows_of(blocks, index):
        return lax.dynamic_index_in_dim(pick(blocks, index), core, 1, keepdims=False)

    def attended_of(whole):
        normed = normalize(whole.reshape(-1, tokens), norm_gain)
        own_half = lax.dot_general(
            normed, keyval_weight, (((0,), (0,)), ((), ())), preferred_element_type=f32
        ).astype(bf16)
        other_half = rotate(own_half, "core", 1)
        queries = lax.dot_general(
            normed, query_weight, (((0,), (0,)), ((), ())), preferred_element_type=f32
        ).astype(bf16)
        block_keys = jnp.where(core == 0, own_half, other_half).reshape(row_count, block_len, HEAD)
        block_values = jnp.where(core == 0, other_half, own_half).reshape(row_count, block_len, HEAD)
        return attend(
            queries.reshape(row_count, block_len, -1, HEAD),
            cache_keys,
            cache_values,
            block_keys,
            block_values,
            prefix_lengths,
        )

    cotangent = lax.all_gather(learner_cotangent, TENSOR, axis=1, tiled=True)
    state = block_states.reshape(tokens, part).T
    whole, _ = gather_rows(pair_order(state, rotate(state, "y", 1), iy, 0), 0)
    attended = attended_of(whole)
    both = jnp.stack([swap_cores(attended), swap_cores(attended, True)])
    attended_all, cotangent = gather_ring(both, cotangent)

    terms = gradient_terms(cotangent.T, learner_inputs)
    halves = lax.psum_scatter(terms, "dp", scatter_dimension=0, tiled=False)
    halves, attended_all = lax.optimization_barrier((halves, attended_all))
    gradient = pick(halves, role).astype(f32) + rotate(pick(halves, 1 - role), "role", 1).astype(f32)
    new_weight, new_first, new_second = adam_update(
        gradient, master_weight.T, first_moment.T, second_moment.T
    )
    weight_part = new_weight.astype(bf16)
    weight_all = lax.all_gather(weight_part, "dp", axis=0)

    place = jnp.stack([role, core]).astype(jnp.int32)
    partial = project_all(
        place,
        weight_part,
        rotate(weight_part, "core", 1),
        attended_all.reshape(4, 2, 2, tokens, depth),
    )
    update = scatter_sum(partial).astype(bf16)

    def deal(flip):
        route = []
        for source in range(256):
            r, d2, d1, d0, x1, x0, y, c = [source >> k & 1 for k in range(7, -1, -1)]
            target = [r ^ x1, d2 ^ x0, d1 ^ y, c, x1, x0, y ^ flip, d0]
            route.append((source, sum(bit << 7 - k for k, bit in enumerate(target))))
        return lax.ppermute(update, EVERY, route)

    shift_x, shift_y = role * 2 + dp // 4, dp // 2 % 2
    update = pair_order(deal(0), deal(1), iy ^ shift_y, 0).astype(f32) * out_scale
    picks = position_picks.reshape(STEPS, 1, tokens)
    rows = revise(rows_of(whole, ix ^ shift_x), update, picks[0], rows_of(masks, ix ^ shift_x))

    whole, weight_all = gather_rows(rows, shift_x, weight_all)
    attended = attended_of(whole)
    near, away = project_own(place, weight_all, attended, rotate(attended, "role", 1))
    partial = (near + rotate(away, "core", 1).astype(f32)).astype(bf16)
    partial = partial.reshape(8, part, tokens)
    update = scatter_sum(partial).astype(bf16)
    update = lax.ppermute(update, ("role", "x1"), [(0, 0), (1, 2), (2, 1), (3, 3)])
    state = pick(rows_of(whole, ix), iy)
    state = revise(state, update.astype(f32) * out_scale, picks[1], pick(rows_of(masks, ix), iy))
    return (state.T.reshape(row_count, block_len, part), new_weight.T, new_first.T, new_second.T)


def solution(mesh):
    fine = Mesh(mesh.devices.reshape(2, 8, 2, 2, 2, 2), EVERY)
    weights = P(TENSOR, RD)
    return jax.shard_map(
        on_device,
        mesh=fine,
        in_specs=(
            P(RD, TENSOR),
            P(RD, TENSOR),
            weights,
            weights,
            weights,
            P(None, TENSOR),
            P(None, TENSOR),
            P(RD, None, TENSOR),
            P(RD, None, TENSOR),
            P(),
            P(),
            P(RD),
            P(None, RD, None),
        ),
        out_specs=(P(RD, None, TENSOR), weights, weights, weights),
        check_vma=False,
    )
```

```python
import jax
import jax.numpy as jnp
from jax import lax
from jax.experimental import pallas as pl
from jax.experimental.pallas import tpu as pltpu
from jax.sharding import Mesh, PartitionSpec as P

HEADS = 64
HEAD = 128
STEPS = 2

BETA_ONE = 0.9
BETA_TWO = 0.95
ADAM_EPS = 1e-08
LEARN_RATE = 0.5
DECAY_RATE = 0.1
STEP_COUNT = 50
NORM_EPS = 1e-06

RD = ("role", "dp")
X = ("x1", "x0")
TENSOR = X + ("y", "core")
EVERY = RD + TENSOR


def rotate(block, axis, shift):
    count = 4 if axis == X else lax.axis_size(axis)
    return lax.ppermute(block, axis, [(low, (low + shift) % count) for low in range(count)])


def pick(blocks, index):
    return lax.dynamic_index_in_dim(blocks, index, 0, keepdims=False)


def pair_order(own, other, index, axis):
    return jnp.where(index == 0, jnp.stack([own, other], axis), jnp.stack([other, own], axis))


def adam_update(gradient, master_weight, first_moment, second_moment):
    first_new = BETA_ONE * first_moment + (1.0 - BETA_ONE) * gradient
    second_new = BETA_TWO * second_moment + (1.0 - BETA_TWO) * gradient * gradient
    first_hat = first_new / (1.0 - BETA_ONE**STEP_COUNT)
    second_hat = second_new / (1.0 - BETA_TWO**STEP_COUNT)
    weight_new = master_weight - LEARN_RATE * (
        first_hat / (jnp.sqrt(second_hat) + ADAM_EPS) + DECAY_RATE * master_weight
    )
    return (weight_new, first_new, second_new)


def gather_rows(rows, shift_x, beside=None):
    ix, ic = lax.axis_index(X), lax.axis_index("core")
    ahead, back, across = rotate(rows, X, 1), rotate(rows, X, -1), rotate(rows, X, 2)
    square = jnp.zeros((4,) + rows.shape, rows.dtype)
    square = lax.dynamic_update_index_in_dim(square, rows, ix ^ shift_x, 0)
    square = lax.dynamic_update_index_in_dim(square, ahead, ((ix + 3) % 4) ^ shift_x, 0)
    square = lax.dynamic_update_index_in_dim(square, back, ((ix + 1) % 4) ^ shift_x, 0)
    square = lax.dynamic_update_index_in_dim(square, across, ((ix + 2) % 4) ^ shift_x, 0)
    square, beside = lax.optimization_barrier((square, beside))
    return pair_order(square, rotate(square, "core", 1), ic, 2), beside


def swap_cores(block, flip_role=False):
    route = []
    for role in range(2):
        for dp in range(8):
            for core in range(2):
                low = dp % 2
                source = (role * 8 + dp) * 2 + core
                target_role = 1 - role if flip_role else role
                target = (target_role * 8 + dp - low + core) * 2 + low
                route.append((source, target))
    return lax.ppermute(block, ("role", "dp", "core"), route)


def gather_ring(block, before):
    me = lax.axis_index("dp")
    high = me - me % 2
    up, down = [block], [block]
    for step in range(3):
        up.append(rotate(up[-1], "dp", 1))
        down.append(rotate(down[-1], "dp", -1))
    before, up, down = lax.optimization_barrier((before, up, down))
    up.append(rotate(up[-1], "dp", 1))
    whole = jnp.zeros((8,) + block.shape, block.dtype)
    for step in range(5):
        whole = lax.dynamic_update_index_in_dim(whole, up[step], ((me + 8 - step) % 8) ^ high, 0)
    for step in range(1, 4):
        whole = lax.dynamic_update_index_in_dim(whole, down[step], ((me + step) % 8) ^ high, 0)
    return whole, before


def scatter_sum(parts):
    blocks = lax.all_to_all(parts, X + ("y",), 0, 0, tiled=True)
    return jnp.sum(blocks.astype(jnp.float32), axis=0)


def gradient_kernel(role_ref, cotangent_ref, inputs_ref, out_ref):
    terms = jnp.dot(cotangent_ref[...], inputs_ref[...], preferred_element_type=jnp.float32)
    out_ref[...] = terms.astype(out_ref.dtype).reshape(out_ref.shape)


def gradient_terms(role, cotangent, inputs):
    tokens, depth = inputs.shape
    part = cotangent.shape[0] // 16
    return pl.pallas_call(
        gradient_kernel,
        grid_spec=pltpu.PrefetchScalarGridSpec(
            num_scalar_prefetch=1,
            grid=(4,),
            in_specs=[
                pl.BlockSpec((4 * part, tokens), lambda i, role: (i, 0)),
                pl.BlockSpec((tokens, depth), lambda i, role: (0, 0)),
            ],
            out_specs=pl.BlockSpec(
                (4, 1, part, depth), lambda i, role: (i % 2, (i // 2) ^ role[0], 0, 0)
            ),
        ),
        out_shape=jax.ShapeDtypeStruct((8, 2, part, depth), jnp.bfloat16),
        compiler_params=pltpu.CompilerParams(vmem_limit_bytes=60 * 1024 * 1024),
        cost_estimate=pl.CostEstimate(
            flops=2 * 16 * part * tokens * depth, bytes_accessed=17_000_000, transcendentals=0
        ),
    )(role, cotangent, inputs)


def contract(weights, tokens):
    dims = (((1,), (1,)), ((), ()))
    total = 0.0
    for weight, values in zip(weights, tokens):
        total += lax.dot_general(weight, values, dims, preferred_element_type=jnp.float32)
    return total.astype(jnp.bfloat16)


def project_all_kernel(place_ref, own_ref, other_ref, tokens_ref, out_ref):
    core = place_ref[1]
    weights = own_ref[...], other_ref[...]
    for n in range(8):
        tokens = [tokens_ref[n % 4, half, n // 4] for half in (core, 1 - core)]
        out_ref[n] = contract(weights, tokens)


def project_all(place, own, other, attended):
    part, depth = own.shape
    tokens = attended.shape[3]
    vmem = pl.BlockSpec(memory_space=pltpu.VMEM)
    return pl.pallas_call(
        project_all_kernel,
        in_specs=[pl.BlockSpec(memory_space=pltpu.SMEM), vmem, vmem, vmem],
        out_specs=vmem,
        out_shape=jax.ShapeDtypeStruct((8, part, tokens), jnp.bfloat16),
        compiler_params=pltpu.CompilerParams(vmem_limit_bytes=32 * 1024 * 1024),
        cost_estimate=pl.CostEstimate(
            flops=32 * part * depth * tokens, bytes_accessed=3_000_000, transcendentals=0
        ),
    )(place, own, other, attended)


def project_own_kernel(place_ref, weight_ref, own_ref, far_ref, near_ref, away_ref):
    role, core = place_ref[0], place_ref[1]
    dims = (((1,), (1,)), ((), ()))
    for tokens_ref, index in ((own_ref, role), (far_ref, 1 - role)):
        tokens = tokens_ref[...]
        near_ref[index, 0] = lax.dot_general(
            weight_ref[core], tokens, dims, preferred_element_type=jnp.float32
        )
        away_ref[index, 0] = contract((weight_ref[1 - core],), (tokens,))


def project_own(place, weight, own, far):
    part, depth = weight.shape[1:]
    tokens = own.shape[0]
    whole = pl.BlockSpec((tokens, depth), lambda k: (0, 0))
    block = pl.BlockSpec((2, 1, part, tokens), lambda k: (0, k, 0, 0))
    return pl.pallas_call(
        project_own_kernel,
        grid=(4,),
        in_specs=[
            pl.BlockSpec(memory_space=pltpu.SMEM),
            pl.BlockSpec((2, part, depth), lambda k: (k, 0, 0)),
            whole,
            whole,
        ],
        out_specs=[block, block],
        out_shape=[
            jax.ShapeDtypeStruct((2, 4, part, tokens), jnp.float32),
            jax.ShapeDtypeStruct((2, 4, part, tokens), jnp.bfloat16),
        ],
        compiler_params=pltpu.CompilerParams(vmem_limit_bytes=32 * 1024 * 1024),
        cost_estimate=pl.CostEstimate(
            flops=32 * part * depth * tokens, bytes_accessed=5_000_000, transcendentals=0
        ),
    )(place, weight, own, far)


def normalize(state, norm_gain):
    values = state.astype(jnp.float32)
    mean_square = jnp.mean(values * values, axis=0, keepdims=True)
    return (values * lax.rsqrt(mean_square + NORM_EPS) * norm_gain[:, None]).astype(jnp.bfloat16)


def revise(current_state, update, pick_codes, mask_values):
    values = current_state.astype(jnp.float32)
    masked = jnp.broadcast_to(mask_values.astype(jnp.float32)[..., None], values.shape)
    return jnp.where(
        pick_codes == 1, values + update, jnp.where(pick_codes == 2, masked, values)
    ).astype(jnp.bfloat16)


def attend(queries, cache_keys, cache_values, block_keys, block_values, prefix_lengths):
    score_scale = HEAD ** (-0.5)
    prefix_len = cache_keys.shape[1]
    prefix_scores = (
        jnp.einsum("rbgh,rph->rgbp", queries, cache_keys, preferred_element_type=jnp.float32)
        * score_scale
    )
    valid_keys = jnp.arange(prefix_len, dtype=jnp.int32)[None, :] < prefix_lengths[:, None]
    prefix_scores = jnp.where(valid_keys[:, None, None, :], prefix_scores, -jnp.inf)
    block_scores = (
        jnp.einsum("rbgh,rch->rgbc", queries, block_keys, preferred_element_type=jnp.float32)
        * score_scale
    )
    score_top = jnp.maximum(jnp.max(prefix_scores, axis=-1), jnp.max(block_scores, axis=-1))[
        ..., None
    ]
    prefix_exp = jnp.exp(prefix_scores - score_top)
    block_exp = jnp.exp(block_scores - score_top)
    denom_sum = (jnp.sum(prefix_exp, axis=-1) + jnp.sum(block_exp, axis=-1))[..., None]
    prefix_probs = (prefix_exp / denom_sum).astype(jnp.bfloat16)
    block_probs = (block_exp / denom_sum).astype(jnp.bfloat16)
    attended = jnp.einsum(
        "rgbp,rph->rbgh", prefix_probs, cache_values, preferred_element_type=jnp.float32
    )
    attended = attended + jnp.einsum(
        "rgbc,rch->rbgh", block_probs, block_values, preferred_element_type=jnp.float32
    )
    return attended.astype(jnp.bfloat16).reshape(queries.shape[0] * queries.shape[1], -1)


def on_device(
    learner_inputs,
    learner_cotangent,
    master_weight,
    first_moment,
    second_moment,
    query_weight,
    keyval_weight,
    prefix_cache,
    block_states,
    norm_gain,
    mask_vector,
    prefix_lengths,
    position_picks,
):
    bf16, f32 = jnp.bfloat16, jnp.float32
    role, core, dp = lax.axis_index("role"), lax.axis_index("core"), lax.axis_index("dp")
    row_count, block_len, part = block_states.shape
    tokens = row_count * block_len
    depth = learner_inputs.shape[1]
    out_scale = (HEADS * HEAD) ** (-0.5)

    cache_other = rotate(prefix_cache, "core", 1)
    cache_keys = jnp.where(core == 0, prefix_cache, cache_other)
    cache_values = jnp.where(core == 0, cache_other, prefix_cache)

    masks = mask_vector.reshape(4, 2, 2, part)
    ix, iy = lax.axis_index(X), lax.axis_index("y")

    def rows_of(blocks, index):
        return lax.dynamic_index_in_dim(pick(blocks, index), core, 1, keepdims=False)

    def attended_of(whole):
        normed = normalize(whole.reshape(-1, tokens), norm_gain)
        own_half = lax.dot_general(
            normed, keyval_weight, (((0,), (0,)), ((), ())), preferred_element_type=f32
        ).astype(bf16)
        other_half = rotate(own_half, "core", 1)
        queries = lax.dot_general(
            normed, query_weight, (((0,), (0,)), ((), ())), preferred_element_type=f32
        ).astype(bf16)
        block_keys = jnp.where(core == 0, own_half, other_half).reshape(row_count, block_len, HEAD)
        block_values = jnp.where(core == 0, other_half, own_half).reshape(row_count, block_len, HEAD)
        return attend(
            queries.reshape(row_count, block_len, -1, HEAD),
            cache_keys,
            cache_values,
            block_keys,
            block_values,
            prefix_lengths,
        )

    cotangent = lax.all_gather(learner_cotangent, TENSOR, axis=1, tiled=True)
    state = block_states.reshape(tokens, part).T
    whole, _ = gather_rows(pair_order(state, rotate(state, "y", 1), iy, 0), 0)
    attended = attended_of(whole)
    both = jnp.stack([swap_cores(attended), swap_cores(attended, True)])
    attended_all, cotangent = gather_ring(both, cotangent)

    terms = gradient_terms(role.astype(jnp.int32).reshape(1), cotangent.T, learner_inputs)
    halves = lax.psum_scatter(terms, "dp", scatter_dimension=0, tiled=False)
    halves, attended_all = lax.optimization_barrier((halves, attended_all))
    halves = halves.reshape(2, part, depth)
    gradient = halves[0].astype(f32) + rotate(halves[1], "role", 1).astype(f32)
    new_weight, new_first, new_second = adam_update(
        gradient, master_weight.T, first_moment.T, second_moment.T
    )
    weight_part = new_weight.astype(bf16)
    weight_sent = lax.optimization_barrier(new_weight).astype(bf16)
    weight_all = lax.all_gather(weight_sent, "dp", axis=0)

    place = jnp.stack([role, core]).astype(jnp.int32)
    partial = project_all(
        place,
        weight_part,
        rotate(weight_part, "core", 1),
        attended_all.reshape(4, 2, 2, tokens, depth),
    )
    update = scatter_sum(partial).astype(bf16)

    def deal(flip):
        route = []
        for source in range(256):
            r, d2, d1, d0, x1, x0, y, c = [source >> k & 1 for k in range(7, -1, -1)]
            target = [r ^ x1, d2 ^ x0, d1 ^ y, c, x1, x0, y ^ flip, d0]
            route.append((source, sum(bit << 7 - k for k, bit in enumerate(target))))
        return lax.ppermute(update, EVERY, route)

    shift_x, shift_y = role * 2 + dp // 4, dp // 2 % 2
    update = pair_order(deal(0), deal(1), iy ^ shift_y, 0).astype(f32) * out_scale
    picks = position_picks.reshape(STEPS, 1, tokens)
    rows = revise(rows_of(whole, ix ^ shift_x), update, picks[0], rows_of(masks, ix ^ shift_x))

    whole, weight_all = gather_rows(rows, shift_x, weight_all)
    attended = attended_of(whole)
    near, away = project_own(place, weight_all, attended, rotate(attended, "role", 1))
    partial = (near + rotate(away, "core", 1).astype(f32)).astype(bf16)
    partial = partial.reshape(8, part, tokens)
    update = scatter_sum(partial).astype(bf16)
    update = lax.ppermute(update, ("role", "x1"), [(0, 0), (1, 2), (2, 1), (3, 3)])
    state = pick(rows_of(whole, ix), iy)
    state = revise(state, update.astype(f32) * out_scale, picks[1], pick(rows_of(masks, ix), iy))
    return (state.T.reshape(row_count, block_len, part), new_weight.T, new_first.T, new_second.T)


def solution(mesh):
    fine = Mesh(mesh.devices.reshape(2, 8, 2, 2, 2, 2), EVERY)
    weights = P(TENSOR, RD)
    return jax.shard_map(
        on_device,
        mesh=fine,
        in_specs=(
            P(RD, TENSOR),
            P(RD, TENSOR),
            weights,
            weights,
            weights,
            P(None, TENSOR),
            P(None, TENSOR),
            P(RD, None, TENSOR),
            P(RD, None, TENSOR),
            P(),
            P(),
            P(RD),
            P(None, RD, None),
        ),
        out_specs=(P(RD, None, TENSOR), weights, weights, weights),
        check_vma=False,
    )
```

```python
import jax
import jax.numpy as jnp
from jax import lax
from jax.experimental import pallas as pl
from jax.experimental.pallas import tpu as pltpu
from jax.sharding import Mesh, PartitionSpec as P

HEADS = 64
HEAD = 128
STEPS = 2

BETA_ONE = 0.9
BETA_TWO = 0.95
ADAM_EPS = 1e-08
LEARN_RATE = 0.5
DECAY_RATE = 0.1
STEP_COUNT = 50
NORM_EPS = 1e-06

RD = ("role", "dp")
X = ("x1", "x0")
TENSOR = X + ("y", "core")
EVERY = RD + TENSOR


def rotate(block, axis, shift):
    count = 4 if axis == X else lax.axis_size(axis)
    return lax.ppermute(block, axis, [(low, (low + shift) % count) for low in range(count)])


def pick(blocks, index):
    return lax.dynamic_index_in_dim(blocks, index, 0, keepdims=False)


def pair_order(own, other, index, axis):
    return jnp.where(index == 0, jnp.stack([own, other], axis), jnp.stack([other, own], axis))


def adam_update(gradient, master_weight, first_moment, second_moment):
    first_new = BETA_ONE * first_moment + (1.0 - BETA_ONE) * gradient
    second_new = BETA_TWO * second_moment + (1.0 - BETA_TWO) * gradient * gradient
    first_hat = first_new / (1.0 - BETA_ONE**STEP_COUNT)
    second_hat = second_new / (1.0 - BETA_TWO**STEP_COUNT)
    weight_new = master_weight - LEARN_RATE * (
        first_hat / (jnp.sqrt(second_hat) + ADAM_EPS) + DECAY_RATE * master_weight
    )
    return (weight_new, first_new, second_new)


def gather_rows(rows, shift_x, beside=None):
    ix, ic = lax.axis_index(X), lax.axis_index("core")
    ahead, back, across = rotate(rows, X, 1), rotate(rows, X, -1), rotate(rows, X, 2)
    square = jnp.zeros((4,) + rows.shape, rows.dtype)
    square = lax.dynamic_update_index_in_dim(square, rows, ix ^ shift_x, 0)
    square = lax.dynamic_update_index_in_dim(square, ahead, ((ix + 3) % 4) ^ shift_x, 0)
    square = lax.dynamic_update_index_in_dim(square, back, ((ix + 1) % 4) ^ shift_x, 0)
    square = lax.dynamic_update_index_in_dim(square, across, ((ix + 2) % 4) ^ shift_x, 0)
    square, beside = lax.optimization_barrier((square, beside))
    return pair_order(square, rotate(square, "core", 1), ic, 2), beside


def swap_cores(block, flip_role=False):
    route = []
    for role in range(2):
        for dp in range(8):
            for core in range(2):
                low = dp % 2
                source = (role * 8 + dp) * 2 + core
                target_role = 1 - role if flip_role else role
                target = (target_role * 8 + dp - low + core) * 2 + low
                route.append((source, target))
    return lax.ppermute(block, ("role", "dp", "core"), route)


def gather_ring(block, before):
    me = lax.axis_index("dp")
    high = me - me % 2
    up, down = [block], [block]
    for step in range(3):
        up.append(rotate(up[-1], "dp", 1))
        down.append(rotate(down[-1], "dp", -1))
    before, up, down = lax.optimization_barrier((before, up, down))
    up.append(rotate(up[-1], "dp", 1))
    whole = jnp.zeros((8,) + block.shape, block.dtype)
    for step in range(5):
        whole = lax.dynamic_update_index_in_dim(whole, up[step], ((me + 8 - step) % 8) ^ high, 0)
    for step in range(1, 4):
        whole = lax.dynamic_update_index_in_dim(whole, down[step], ((me + step) % 8) ^ high, 0)
    return whole, before


def scatter_sum(parts):
    blocks = lax.all_to_all(parts, X + ("y",), 0, 0, tiled=True)
    return jnp.sum(blocks.astype(jnp.float32), axis=0)


def gradient_kernel(role_ref, cotangent_ref, inputs_ref, out_ref):
    terms = jnp.dot(cotangent_ref[...], inputs_ref[...], preferred_element_type=jnp.float32)
    out_ref[...] = terms.astype(out_ref.dtype).reshape(out_ref.shape)


def gradient_terms(role, cotangent, inputs):
    tokens, depth = inputs.shape
    part = cotangent.shape[0] // 16
    return pl.pallas_call(
        gradient_kernel,
        grid_spec=pltpu.PrefetchScalarGridSpec(
            num_scalar_prefetch=1,
            grid=(4,),
            in_specs=[
                pl.BlockSpec((4 * part, tokens), lambda i, role: (i, 0)),
                pl.BlockSpec((tokens, depth), lambda i, role: (0, 0)),
            ],
            out_specs=pl.BlockSpec(
                (4, 1, part, depth), lambda i, role: (i % 2, (i // 2) ^ role[0], 0, 0)
            ),
        ),
        out_shape=jax.ShapeDtypeStruct((8, 2, part, depth), jnp.bfloat16),
        compiler_params=pltpu.CompilerParams(vmem_limit_bytes=60 * 1024 * 1024),
        cost_estimate=pl.CostEstimate(
            flops=2 * 16 * part * tokens * depth, bytes_accessed=17_000_000, transcendentals=0
        ),
    )(role, cotangent, inputs)


def contract(weights, tokens):
    dims = (((1,), (1,)), ((), ()))
    total = 0.0
    for weight, values in zip(weights, tokens):
        total += lax.dot_general(weight, values, dims, preferred_element_type=jnp.float32)
    return total.astype(jnp.bfloat16)


def project_all_kernel(place_ref, own_ref, other_ref, tokens_ref, out_ref):
    core = place_ref[1]
    weights = own_ref[...], other_ref[...]
    for n in range(8):
        tokens = [tokens_ref[n % 4, half, n // 4] for half in (core, 1 - core)]
        out_ref[n] = contract(weights, tokens)


def project_all(place, own, other, attended):
    part, depth = own.shape
    tokens = attended.shape[3]
    vmem = pl.BlockSpec(memory_space=pltpu.VMEM)
    return pl.pallas_call(
        project_all_kernel,
        in_specs=[pl.BlockSpec(memory_space=pltpu.SMEM), vmem, vmem, vmem],
        out_specs=vmem,
        out_shape=jax.ShapeDtypeStruct((8, part, tokens), jnp.bfloat16),
        compiler_params=pltpu.CompilerParams(vmem_limit_bytes=32 * 1024 * 1024),
        cost_estimate=pl.CostEstimate(
            flops=32 * part * depth * tokens, bytes_accessed=3_000_000, transcendentals=0
        ),
    )(place, own, other, attended)


def project_own_kernel(place_ref, weight_ref, own_ref, far_ref, near_ref, away_ref):
    role, core = place_ref[0], place_ref[1]
    dims = (((1,), (1,)), ((), ()))
    for tokens_ref, index in ((own_ref, role), (far_ref, 1 - role)):
        tokens = tokens_ref[...]
        near_ref[index, 0] = lax.dot_general(
            weight_ref[core], tokens, dims, preferred_element_type=jnp.float32
        )
        away_ref[index, 0] = contract((weight_ref[1 - core],), (tokens,))


def project_own(place, weight, own, far):
    part, depth = weight.shape[1:]
    tokens = own.shape[0]
    whole = pl.BlockSpec((tokens, depth), lambda k: (0, 0))
    block = pl.BlockSpec((2, 1, part, tokens), lambda k: (0, k, 0, 0))
    return pl.pallas_call(
        project_own_kernel,
        grid=(4,),
        in_specs=[
            pl.BlockSpec(memory_space=pltpu.SMEM),
            pl.BlockSpec((2, part, depth), lambda k: (k, 0, 0)),
            whole,
            whole,
        ],
        out_specs=[block, block],
        out_shape=[
            jax.ShapeDtypeStruct((2, 4, part, tokens), jnp.float32),
            jax.ShapeDtypeStruct((2, 4, part, tokens), jnp.bfloat16),
        ],
        compiler_params=pltpu.CompilerParams(vmem_limit_bytes=32 * 1024 * 1024),
        cost_estimate=pl.CostEstimate(
            flops=32 * part * depth * tokens, bytes_accessed=5_000_000, transcendentals=0
        ),
    )(place, weight, own, far)


def normalize(state, norm_gain):
    values = state.astype(jnp.float32)
    mean_square = jnp.mean(values * values, axis=0, keepdims=True)
    return (values * lax.rsqrt(mean_square + NORM_EPS) * norm_gain[:, None]).astype(jnp.bfloat16)


def revise(current_state, update, pick_codes, mask_values):
    values = current_state.astype(jnp.float32)
    masked = jnp.broadcast_to(mask_values.astype(jnp.float32)[..., None], values.shape)
    return jnp.where(
        pick_codes == 1, values + update, jnp.where(pick_codes == 2, masked, values)
    ).astype(jnp.bfloat16)


def attend(queries, cache_keys, cache_values, block_keys, block_values, prefix_lengths):
    score_scale = HEAD ** (-0.5)
    prefix_len = cache_keys.shape[1]
    prefix_scores = (
        jnp.einsum("rbgh,rph->rgbp", queries, cache_keys, preferred_element_type=jnp.float32)
        * score_scale
    )
    valid_keys = jnp.arange(prefix_len, dtype=jnp.int32)[None, :] < prefix_lengths[:, None]
    prefix_scores = jnp.where(valid_keys[:, None, None, :], prefix_scores, -jnp.inf)
    block_scores = (
        jnp.einsum("rbgh,rch->rgbc", queries, block_keys, preferred_element_type=jnp.float32)
        * score_scale
    )
    score_top = jnp.maximum(jnp.max(prefix_scores, axis=-1), jnp.max(block_scores, axis=-1))[
        ..., None
    ]
    prefix_exp = jnp.exp(prefix_scores - score_top)
    block_exp = jnp.exp(block_scores - score_top)
    denom_sum = (jnp.sum(prefix_exp, axis=-1) + jnp.sum(block_exp, axis=-1))[..., None]
    prefix_probs = (prefix_exp / denom_sum).astype(jnp.bfloat16)
    block_probs = (block_exp / denom_sum).astype(jnp.bfloat16)
    attended = jnp.einsum(
        "rgbp,rph->rbgh", prefix_probs, cache_values, preferred_element_type=jnp.float32
    )
    attended = attended + jnp.einsum(
        "rgbc,rch->rbgh", block_probs, block_values, preferred_element_type=jnp.float32
    )
    return attended.astype(jnp.bfloat16).reshape(queries.shape[0] * queries.shape[1], -1)


def on_device(
    learner_inputs,
    learner_cotangent,
    master_weight,
    first_moment,
    second_moment,
    query_weight,
    keyval_weight,
    prefix_cache,
    block_states,
    norm_gain,
    mask_vector,
    prefix_lengths,
    position_picks,
):
    bf16, f32 = jnp.bfloat16, jnp.float32
    role, core, dp = lax.axis_index("role"), lax.axis_index("core"), lax.axis_index("dp")
    row_count, block_len, part = block_states.shape
    tokens = row_count * block_len
    depth = learner_inputs.shape[1]
    out_scale = (HEADS * HEAD) ** (-0.5)

    cache_other = rotate(prefix_cache, "core", 1)
    cache_keys = jnp.where(core == 0, prefix_cache, cache_other)
    cache_values = jnp.where(core == 0, cache_other, prefix_cache)

    masks = mask_vector.reshape(4, 2, 2, part)
    ix, iy = lax.axis_index(X), lax.axis_index("y")

    def rows_of(blocks, index):
        return lax.dynamic_index_in_dim(pick(blocks, index), core, 1, keepdims=False)

    def attended_of(whole):
        normed = normalize(whole.reshape(-1, tokens), norm_gain)
        own_half = lax.dot_general(
            normed, keyval_weight, (((0,), (0,)), ((), ())), preferred_element_type=f32
        ).astype(bf16)
        other_half = rotate(own_half, "core", 1)
        queries = lax.dot_general(
            normed, query_weight, (((0,), (0,)), ((), ())), preferred_element_type=f32
        ).astype(bf16)
        block_keys = jnp.where(core == 0, own_half, other_half).reshape(row_count, block_len, HEAD)
        block_values = jnp.where(core == 0, other_half, own_half).reshape(row_count, block_len, HEAD)
        return attend(
            queries.reshape(row_count, block_len, -1, HEAD),
            cache_keys,
            cache_values,
            block_keys,
            block_values,
            prefix_lengths,
        )

    cotangent = lax.all_gather(learner_cotangent, TENSOR, axis=1, tiled=True)
    state = block_states.reshape(tokens, part).T
    whole, _ = gather_rows(pair_order(state, rotate(state, "y", 1), iy, 0), 0)
    attended = attended_of(whole)
    both = jnp.stack([swap_cores(attended), swap_cores(attended, True)])
    attended_all, cotangent = gather_ring(both, cotangent)

    terms = gradient_terms(role.astype(jnp.int32).reshape(1), cotangent.T, learner_inputs)
    halves = lax.psum_scatter(terms, "dp", scatter_dimension=0, tiled=False)
    halves, attended_all = lax.optimization_barrier((halves, attended_all))
    halves = halves.reshape(2, part, depth)
    gradient = halves[0].astype(f32) + rotate(halves[1], "role", 1).astype(f32)
    new_weight, new_first, new_second = adam_update(
        gradient, master_weight.T, first_moment.T, second_moment.T
    )
    weight_part = new_weight.astype(bf16)
    weight_all = lax.all_gather(weight_part, "dp", axis=0)

    place = jnp.stack([role, core]).astype(jnp.int32)
    partial = project_all(
        place,
        weight_part,
        rotate(weight_part, "core", 1),
        attended_all.reshape(4, 2, 2, tokens, depth),
    )
    update = scatter_sum(partial).astype(bf16)

    def deal(flip):
        route = []
        for source in range(256):
            r, d2, d1, d0, x1, x0, y, c = [source >> k & 1 for k in range(7, -1, -1)]
            target = [r ^ x1, d2 ^ x0, d1 ^ y, c, x1, x0, y ^ flip, d0]
            route.append((source, sum(bit << 7 - k for k, bit in enumerate(target))))
        return lax.ppermute(update, EVERY, route)

    shift_x, shift_y = role * 2 + dp // 4, dp // 2 % 2
    update = pair_order(deal(0), deal(1), iy ^ shift_y, 0).astype(f32) * out_scale
    picks = position_picks.reshape(STEPS, 1, tokens)
    rows = revise(rows_of(whole, ix ^ shift_x), update, picks[0], rows_of(masks, ix ^ shift_x))

    whole, weight_all = gather_rows(rows, shift_x, weight_all)
    attended = attended_of(whole)
    near, away = project_own(place, weight_all, attended, rotate(attended, "role", 1))
    partial = (near + rotate(away, "core", 1).astype(f32)).astype(bf16)
    partial = partial.reshape(8, part, tokens)
    update = scatter_sum(partial).astype(bf16)
    update = lax.ppermute(update, ("role", "x1"), [(0, 0), (1, 2), (2, 1), (3, 3)])
    state = pick(rows_of(whole, ix), iy)
    state = revise(state, update.astype(f32) * out_scale, picks[1], pick(rows_of(masks, ix), iy))
    return (state.T.reshape(row_count, block_len, part), new_weight.T, new_first.T, new_second.T)


def solution(mesh):
    fine = Mesh(mesh.devices.reshape(2, 8, 2, 2, 2, 2), EVERY)
    weights = P(TENSOR, RD)
    return jax.shard_map(
        on_device,
        mesh=fine,
        in_specs=(
            P(RD, TENSOR),
            P(RD, TENSOR),
            weights,
            weights,
            weights,
            P(None, TENSOR),
            P(None, TENSOR),
            P(RD, None, TENSOR),
            P(RD, None, TENSOR),
            P(),
            P(),
            P(RD),
            P(None, RD, None),
        ),
        out_specs=(P(RD, None, TENSOR), weights, weights, weights),
        check_vma=False,
    )
```

```python
import jax
import jax.numpy as jnp
from jax import lax
from jax.experimental import pallas as pl
from jax.experimental.pallas import tpu as pltpu
from jax.sharding import Mesh, PartitionSpec as P

HEADS = 64
HEAD = 128
STEPS = 2

BETA_ONE = 0.9
BETA_TWO = 0.95
ADAM_EPS = 1e-08
LEARN_RATE = 0.5
DECAY_RATE = 0.1
STEP_COUNT = 50
NORM_EPS = 1e-06

RD = ("role", "dp")
X = ("x1", "x0")
TENSOR = X + ("y", "core")
EVERY = RD + TENSOR


def rotate(block, axis, shift):
    count = 4 if axis == X else lax.axis_size(axis)
    return lax.ppermute(block, axis, [(low, (low + shift) % count) for low in range(count)])


def pick(blocks, index):
    return lax.dynamic_index_in_dim(blocks, index, 0, keepdims=False)


def pair_order(own, other, index, axis):
    return jnp.where(index == 0, jnp.stack([own, other], axis), jnp.stack([other, own], axis))


def adam_update(gradient, master_weight, first_moment, second_moment):
    first_new = BETA_ONE * first_moment + (1.0 - BETA_ONE) * gradient
    second_new = BETA_TWO * second_moment + (1.0 - BETA_TWO) * gradient * gradient
    first_hat = first_new / (1.0 - BETA_ONE**STEP_COUNT)
    second_hat = second_new / (1.0 - BETA_TWO**STEP_COUNT)
    weight_new = master_weight - LEARN_RATE * (
        first_hat / (jnp.sqrt(second_hat) + ADAM_EPS) + DECAY_RATE * master_weight
    )
    return (weight_new, first_new, second_new)


def gather_rows(rows, shift_x, beside=None):
    ix, ic = lax.axis_index(X), lax.axis_index("core")
    ahead, back, across = rotate(rows, X, 1), rotate(rows, X, -1), rotate(rows, X, 2)
    square = jnp.zeros((4,) + rows.shape, rows.dtype)
    square = lax.dynamic_update_index_in_dim(square, rows, ix ^ shift_x, 0)
    square = lax.dynamic_update_index_in_dim(square, ahead, ((ix + 3) % 4) ^ shift_x, 0)
    square = lax.dynamic_update_index_in_dim(square, back, ((ix + 1) % 4) ^ shift_x, 0)
    square = lax.dynamic_update_index_in_dim(square, across, ((ix + 2) % 4) ^ shift_x, 0)
    square, beside = lax.optimization_barrier((square, beside))
    return pair_order(square, rotate(square, "core", 1), ic, 2), beside


def swap_cores(block, flip_role=False):
    route = []
    for role in range(2):
        for dp in range(8):
            for core in range(2):
                low = dp % 2
                source = (role * 8 + dp) * 2 + core
                target_role = 1 - role if flip_role else role
                target = (target_role * 8 + dp - low + core) * 2 + low
                route.append((source, target))
    return lax.ppermute(block, ("role", "dp", "core"), route)


def gather_ring(block, before):
    me = lax.axis_index("dp")
    high = me - me % 2
    up, down = [block], [block]
    for step in range(3):
        up.append(rotate(up[-1], "dp", 1))
        down.append(rotate(down[-1], "dp", -1))
    before, up, down = lax.optimization_barrier((before, up, down))
    up.append(rotate(up[-1], "dp", 1))
    whole = jnp.zeros((8,) + block.shape, block.dtype)
    for step in range(5):
        whole = lax.dynamic_update_index_in_dim(whole, up[step], ((me + 8 - step) % 8) ^ high, 0)
    for step in range(1, 4):
        whole = lax.dynamic_update_index_in_dim(whole, down[step], ((me + step) % 8) ^ high, 0)
    return whole, before


def scatter_sum(parts):
    blocks = lax.all_to_all(parts, X + ("y",), 0, 0, tiled=True)
    return jnp.sum(blocks.astype(jnp.float32), axis=0)


def gradient_kernel(role_ref, cotangent_ref, inputs_ref, out_ref):
    terms = jnp.dot(cotangent_ref[...], inputs_ref[...], preferred_element_type=jnp.float32)
    out_ref[...] = terms.astype(out_ref.dtype).reshape(out_ref.shape)


def gradient_terms(role, cotangent, inputs):
    tokens, depth = inputs.shape
    part = cotangent.shape[0] // 16
    return pl.pallas_call(
        gradient_kernel,
        grid_spec=pltpu.PrefetchScalarGridSpec(
            num_scalar_prefetch=1,
            grid=(4,),
            in_specs=[
                pl.BlockSpec((4 * part, tokens), lambda i, role: (i, 0)),
                pl.BlockSpec((tokens, depth), lambda i, role: (0, 0)),
            ],
            out_specs=pl.BlockSpec(
                (4, 1, part, depth), lambda i, role: (i % 2, (i // 2) ^ role[0], 0, 0)
            ),
        ),
        out_shape=jax.ShapeDtypeStruct((8, 2, part, depth), jnp.bfloat16),
        compiler_params=pltpu.CompilerParams(vmem_limit_bytes=60 * 1024 * 1024),
        cost_estimate=pl.CostEstimate(
            flops=2 * 16 * part * tokens * depth, bytes_accessed=17_000_000, transcendentals=0
        ),
    )(role, cotangent, inputs)


def contract(weights, tokens):
    dims = (((1,), (1,)), ((), ()))
    total = 0.0
    for weight, values in zip(weights, tokens):
        total += lax.dot_general(weight, values, dims, preferred_element_type=jnp.float32)
    return total.astype(jnp.bfloat16)


def project_all_kernel(
    place_ref, own_ref, other_ref, tokens_ref, out_ref, weights, tokens, outs, in_sems, out_sems
):
    core = place_ref[1]
    reads = [
        pltpu.make_async_copy(own_ref, weights.at[0], in_sems.at[0]),
        pltpu.make_async_copy(other_ref, weights.at[1], in_sems.at[1]),
    ]
    for k in range(4):
        reads.append(pltpu.make_async_copy(tokens_ref.at[k], tokens.at[k], in_sems.at[2 + k]))
    for copy in reads:
        copy.start()
    reads[0].wait()
    reads[1].wait()
    copies = []
    for k in range(4):
        reads[2 + k].wait()
        for r in range(2):
            n = r * 4 + k
            values = [tokens[k, half, r] for half in (core, 1 - core)]
            outs[n] = contract((weights[0], weights[1]), values)
            copies.append(pltpu.make_async_copy(outs.at[n], out_ref.at[n], out_sems.at[n]))
            copies[-1].start()
    for copy in copies:
        copy.wait()


def project_all(place, own, other, attended):
    part, depth = own.shape
    tokens = attended.shape[3]
    anywhere = pl.BlockSpec(memory_space=pl.ANY)
    return pl.pallas_call(
        project_all_kernel,
        in_specs=[pl.BlockSpec(memory_space=pltpu.SMEM), anywhere, anywhere, anywhere],
        out_specs=anywhere,
        out_shape=jax.ShapeDtypeStruct((8, part, tokens), jnp.bfloat16),
        scratch_shapes=[
            pltpu.VMEM((2, part, depth), jnp.bfloat16),
            pltpu.VMEM(attended.shape, jnp.bfloat16),
            pltpu.VMEM((8, part, tokens), jnp.bfloat16),
            pltpu.SemaphoreType.DMA((6,)),
            pltpu.SemaphoreType.DMA((8,)),
        ],
        compiler_params=pltpu.CompilerParams(vmem_limit_bytes=60 * 1024 * 1024),
        cost_estimate=pl.CostEstimate(
            flops=32 * part * depth * tokens, bytes_accessed=3_000_000, transcendentals=0
        ),
    )(place, own, other, attended)


def project_own_kernel(place_ref, weight_ref, own_ref, far_ref, near_ref, away_ref):
    role, core = place_ref[0], place_ref[1]
    dims = (((1,), (1,)), ((), ()))
    for tokens_ref, index in ((own_ref, role), (far_ref, 1 - role)):
        tokens = tokens_ref[...]
        near_ref[index, 0] = lax.dot_general(
            weight_ref[core], tokens, dims, preferred_element_type=jnp.float32
        )
        away_ref[index, 0] = contract((weight_ref[1 - core],), (tokens,))


def project_own(place, weight, own, far):
    part, depth = weight.shape[1:]
    tokens = own.shape[0]
    whole = pl.BlockSpec((tokens, depth), lambda k: (0, 0))
    block = pl.BlockSpec((2, 1, part, tokens), lambda k: (0, k, 0, 0))
    return pl.pallas_call(
        project_own_kernel,
        grid=(4,),
        in_specs=[
            pl.BlockSpec(memory_space=pltpu.SMEM),
            pl.BlockSpec((2, part, depth), lambda k: (k, 0, 0)),
            whole,
            whole,
        ],
        out_specs=[block, block],
        out_shape=[
            jax.ShapeDtypeStruct((2, 4, part, tokens), jnp.float32),
            jax.ShapeDtypeStruct((2, 4, part, tokens), jnp.bfloat16),
        ],
        compiler_params=pltpu.CompilerParams(vmem_limit_bytes=32 * 1024 * 1024),
        cost_estimate=pl.CostEstimate(
            flops=32 * part * depth * tokens, bytes_accessed=5_000_000, transcendentals=0
        ),
    )(place, weight, own, far)


def normalize(state, norm_gain):
    values = state.astype(jnp.float32)
    mean_square = jnp.mean(values * values, axis=0, keepdims=True)
    return (values * lax.rsqrt(mean_square + NORM_EPS) * norm_gain[:, None]).astype(jnp.bfloat16)


def revise(current_state, update, pick_codes, mask_values):
    values = current_state.astype(jnp.float32)
    masked = jnp.broadcast_to(mask_values.astype(jnp.float32)[..., None], values.shape)
    return jnp.where(
        pick_codes == 1, values + update, jnp.where(pick_codes == 2, masked, values)
    ).astype(jnp.bfloat16)


def attend(queries, cache_keys, cache_values, block_keys, block_values, prefix_lengths):
    score_scale = HEAD ** (-0.5)
    prefix_len = cache_keys.shape[1]
    prefix_scores = (
        jnp.einsum("rbgh,rph->rgbp", queries, cache_keys, preferred_element_type=jnp.float32)
        * score_scale
    )
    valid_keys = jnp.arange(prefix_len, dtype=jnp.int32)[None, :] < prefix_lengths[:, None]
    prefix_scores = jnp.where(valid_keys[:, None, None, :], prefix_scores, -jnp.inf)
    block_scores = (
        jnp.einsum("rbgh,rch->rgbc", queries, block_keys, preferred_element_type=jnp.float32)
        * score_scale
    )
    score_top = jnp.maximum(jnp.max(prefix_scores, axis=-1), jnp.max(block_scores, axis=-1))[
        ..., None
    ]
    prefix_exp = jnp.exp(prefix_scores - score_top)
    block_exp = jnp.exp(block_scores - score_top)
    denom_sum = (jnp.sum(prefix_exp, axis=-1) + jnp.sum(block_exp, axis=-1))[..., None]
    prefix_probs = (prefix_exp / denom_sum).astype(jnp.bfloat16)
    block_probs = (block_exp / denom_sum).astype(jnp.bfloat16)
    attended = jnp.einsum(
        "rgbp,rph->rbgh", prefix_probs, cache_values, preferred_element_type=jnp.float32
    )
    attended = attended + jnp.einsum(
        "rgbc,rch->rbgh", block_probs, block_values, preferred_element_type=jnp.float32
    )
    return attended.astype(jnp.bfloat16).reshape(queries.shape[0] * queries.shape[1], -1)


def on_device(
    learner_inputs,
    learner_cotangent,
    master_weight,
    first_moment,
    second_moment,
    query_weight,
    keyval_weight,
    prefix_cache,
    block_states,
    norm_gain,
    mask_vector,
    prefix_lengths,
    position_picks,
):
    bf16, f32 = jnp.bfloat16, jnp.float32
    role, core, dp = lax.axis_index("role"), lax.axis_index("core"), lax.axis_index("dp")
    row_count, block_len, part = block_states.shape
    tokens = row_count * block_len
    depth = learner_inputs.shape[1]
    out_scale = (HEADS * HEAD) ** (-0.5)

    cache_other = rotate(prefix_cache, "core", 1)
    cache_keys = jnp.where(core == 0, prefix_cache, cache_other)
    cache_values = jnp.where(core == 0, cache_other, prefix_cache)

    masks = mask_vector.reshape(4, 2, 2, part)
    ix, iy = lax.axis_index(X), lax.axis_index("y")

    def rows_of(blocks, index):
        return lax.dynamic_index_in_dim(pick(blocks, index), core, 1, keepdims=False)

    def attended_of(whole):
        normed = normalize(whole.reshape(-1, tokens), norm_gain)
        own_half = lax.dot_general(
            normed, keyval_weight, (((0,), (0,)), ((), ())), preferred_element_type=f32
        ).astype(bf16)
        other_half = rotate(own_half, "core", 1)
        queries = lax.dot_general(
            normed, query_weight, (((0,), (0,)), ((), ())), preferred_element_type=f32
        ).astype(bf16)
        block_keys = jnp.where(core == 0, own_half, other_half).reshape(row_count, block_len, HEAD)
        block_values = jnp.where(core == 0, other_half, own_half).reshape(row_count, block_len, HEAD)
        return attend(
            queries.reshape(row_count, block_len, -1, HEAD),
            cache_keys,
            cache_values,
            block_keys,
            block_values,
            prefix_lengths,
        )

    cotangent = lax.all_gather(learner_cotangent, TENSOR, axis=1, tiled=True)
    state = block_states.reshape(tokens, part).T
    whole, _ = gather_rows(pair_order(state, rotate(state, "y", 1), iy, 0), 0)
    attended = attended_of(whole)
    both = jnp.stack([swap_cores(attended), swap_cores(attended, True)])
    attended_all, cotangent = gather_ring(both, cotangent)

    terms = gradient_terms(role.astype(jnp.int32).reshape(1), cotangent.T, learner_inputs)
    halves = lax.psum_scatter(terms, "dp", scatter_dimension=0, tiled=False)
    halves, attended_all = lax.optimization_barrier((halves, attended_all))
    halves = halves.reshape(2, part, depth)
    gradient = halves[0].astype(f32) + rotate(halves[1], "role", 1).astype(f32)
    new_weight, new_first, new_second = adam_update(
        gradient, master_weight.T, first_moment.T, second_moment.T
    )
    weight_part = new_weight.astype(bf16)
    weight_all = lax.all_gather(weight_part, "dp", axis=0)

    place = jnp.stack([role, core]).astype(jnp.int32)
    partial = project_all(
        place,
        weight_part,
        rotate(weight_part, "core", 1),
        attended_all.reshape(4, 2, 2, tokens, depth),
    )
    update = scatter_sum(partial).astype(bf16)

    def deal(flip):
        route = []
        for source in range(256):
            r, d2, d1, d0, x1, x0, y, c = [source >> k & 1 for k in range(7, -1, -1)]
            target = [r ^ x1, d2 ^ x0, d1 ^ y, c, x1, x0, y ^ flip, d0]
            route.append((source, sum(bit << 7 - k for k, bit in enumerate(target))))
        return lax.ppermute(update, EVERY, route)

    shift_x, shift_y = role * 2 + dp // 4, dp // 2 % 2
    update = pair_order(deal(0), deal(1), iy ^ shift_y, 0).astype(f32) * out_scale
    picks = position_picks.reshape(STEPS, 1, tokens)
    rows = revise(rows_of(whole, ix ^ shift_x), update, picks[0], rows_of(masks, ix ^ shift_x))

    whole, weight_all = gather_rows(rows, shift_x, weight_all)
    attended = attended_of(whole)
    near, away = project_own(place, weight_all, attended, rotate(attended, "role", 1))
    partial = (near + rotate(away, "core", 1).astype(f32)).astype(bf16)
    partial = partial.reshape(8, part, tokens)
    update = scatter_sum(partial).astype(bf16)
    update = lax.ppermute(update, ("role", "x1"), [(0, 0), (1, 2), (2, 1), (3, 3)])
    state = pick(rows_of(whole, ix), iy)
    state = revise(state, update.astype(f32) * out_scale, picks[1], pick(rows_of(masks, ix), iy))
    return (state.T.reshape(row_count, block_len, part), new_weight.T, new_first.T, new_second.T)


def solution(mesh):
    fine = Mesh(mesh.devices.reshape(2, 8, 2, 2, 2, 2), EVERY)
    weights = P(TENSOR, RD)
    return jax.shard_map(
        on_device,
        mesh=fine,
        in_specs=(
            P(RD, TENSOR),
            P(RD, TENSOR),
            weights,
            weights,
            weights,
            P(None, TENSOR),
            P(None, TENSOR),
            P(RD, None, TENSOR),
            P(RD, None, TENSOR),
            P(),
            P(),
            P(RD),
            P(None, RD, None),
        ),
        out_specs=(P(RD, None, TENSOR), weights, weights, weights),
        check_vma=False,
    )
```
